128 devices in a mesh: seq: 64 (over z_lo, x, y, core), dp: 2 (over z_hi).
Axes of the slice: x: 4, y: 4, z: 4 (z_hi: 2, z_lo: 2; z = z_hi * 2 + z_lo), core: 2. Of those that a mesh axis runs over, the one named last changes fastest.
Arguments:
- tokens: bfloat16 [2, 8192, 4096], P('dp', 'seq'), may hold values from -6 to 6
- queries: bfloat16 [2, 8192, 4096], P('dp', 'seq'), may hold values from -6 to 6
- keys: bfloat16 [2, 8192, 4096], P('dp', 'seq'), may hold values from -6 to 6
- values: bfloat16 [2, 8192, 4096], P('dp', 'seq'), may hold values from -6 to 6
- upstream: bfloat16 [2, 8192, 4096], P('dp', 'seq'), may hold values from -0.15625 to 0.15625
- filters: float32 [8192, 4096], P(None, 'seq'), may hold values from -4 to 4
Outputs:
- update: float32 [64, 512, 1024], P('seq', None, 'dp')
- filter_grad: float32 [8192, 4096], P('dp', 'seq')
The draws below stay inside these ranges and needn't reach their ends.
All inputs are finite; a program needn't handle non-finite values.
Results may differ from the reference program's by a relative error of at most 0.0006.
The reference program's roundings to bfloat16 on the way (of `conv_grad`, `gate_input` and `back_grad`) count: a program that leaves them out, or rounds other values in their place, can miss the bound.
Values may be sent and summed in bfloat16 or wider, within the bound.
A program may use at most 192 MiB of HBM per device.

```python
import math
import jax
import jax.numpy as jnp
from jax import lax

D = 4096
C = 4096
ROW_BLOCKS = 8
NS_STEPS = 5
LENGTH = 8192
SEQS = 2
COL_BLOCKS = 8
BLOCK_ROWS = 512
BLOCK_COLS = 1024
N_SEQ = 64


def draw_filters(key, part):
    key = jax.random.fold_in(key, 7)
    decay_key, random_key = jax.random.split(key)
    slowest = math.log(0.5 * math.log(10.0) / LENGTH)
    fastest = math.log(1.0 / 30.0)
    decays = jnp.exp(jax.random.uniform(decay_key, (C,), jnp.float32, slowest, fastest))
    random_part = jax.random.truncated_normal(random_key, -4.0, 4.0, (LENGTH, C), jnp.float32)
    positions = jnp.arange(LENGTH, dtype=jnp.float32)[:, None]
    energy = (1.0 - jnp.exp(-2.0 * decays * LENGTH)) / (1.0 - jnp.exp(-2.0 * decays))
    return random_part * jnp.exp(-positions * decays[None, :]) / jnp.sqrt(energy)[None, :]


def block_levels(key, dims, cuts, low, largest):
    def one(axis_at, shards_of):
        draws = jax.random.uniform(jax.random.fold_in(jax.random.fold_in(key, 6), axis_at), (shards_of,), jnp.float32, low / len(cuts), largest / len(cuts))
        return jnp.repeat(jnp.exp(draws), dims[axis_at] // shards_of).reshape((-1,) + (1,) * (len(dims) - axis_at - 1))

    loudness = one(*cuts[0])
    for cut in cuts[1:]:
        loudness = loudness * one(*cut)
    return loudness


def normal_values(stream_key, dims, spread, most, shards=(), kind=jnp.bfloat16):
    array = jax.random.normal(stream_key, dims, jnp.float32) * spread
    if len(shards) > 0:
        array = block_levels(stream_key, dims, shards, -0.22, 0.18) * array
    return jnp.clip(array, min=-most, max=most).astype(kind)


def setup_inputs(seed: int = 0) -> dict:
    arg_keys = jax.random.split(jax.random.key(seed), 7)
    return {
        "tokens": normal_values(arg_keys[0], (SEQS, LENGTH, D), 1.0, 6.0, ((0, 2), (1, 64))),
        "queries": normal_values(arg_keys[1], (SEQS, LENGTH, C), 1.0, 6.0, ((0, 2), (1, 64))),
        "keys": normal_values(arg_keys[2], (SEQS, LENGTH, C), 1.0, 6.0, ((0, 2), (1, 64))),
        "values": normal_values(arg_keys[3], (SEQS, LENGTH, C), 1.0, 6.0, ((0, 2), (1, 64))),
        "upstream": normal_values(arg_keys[4], (SEQS, LENGTH, C), (LENGTH ** -0.5), 0.15625, ((0, 2), (1, 64))),
        "filters": draw_filters(jax.random.fold_in(arg_keys[6], 71), 0),
    }


COEF_A = 3.4445
COEF_B = -4.775
COEF_C = 2.0315

def orthogonalize(blocks):
    norms = jnp.sqrt(lax.optimization_barrier(jnp.sum(blocks * blocks, axis=(1, 2), keepdims=True)))
    current = blocks / (norms + 1e-07)
    for iteration in range(NS_STEPS):
        gram = jnp.einsum('sij,skj->sik', current, current, precision=lax.Precision.HIGHEST)
        square = jnp.einsum('sij,sjk->sik', gram, gram, precision=lax.Precision.HIGHEST)
        mixer = COEF_B * gram + COEF_C * square
        product = jnp.einsum('sij,sjk->sik', mixer, current, precision=lax.Precision.HIGHEST)
        current = COEF_A * current + product
    return current

def reference(tokens, queries, keys, values, upstream, filters):
    padded_len = 2 * LENGTH
    filter_spec = jnp.fft.rfft(filters, n=padded_len, axis=0)
    weight_grad = jnp.zeros((D, 2 * C), jnp.float32)
    filter_grad = jnp.zeros((LENGTH, C), jnp.float32)
    for sequence in range(SEQS):
        key_wide = keys[sequence].astype(jnp.float32)
        value_wide = values[sequence].astype(jnp.float32)
        conv_grad = (upstream[sequence].astype(jnp.float32) * queries[sequence].astype(jnp.float32)).astype(jnp.bfloat16)
        gate_input = (key_wide * value_wide).astype(jnp.bfloat16)
        grad_spec = jnp.fft.rfft(conv_grad.astype(jnp.float32), n=padded_len, axis=0)
        input_spec = jnp.fft.rfft(gate_input.astype(jnp.float32), n=padded_len, axis=0)
        back_grad = jnp.fft.irfft(jnp.conj(filter_spec) * grad_spec, n=padded_len, axis=0)[:LENGTH]
        back_grad = back_grad.astype(jnp.float32).astype(jnp.bfloat16)
        filter_term = jnp.fft.irfft(grad_spec * jnp.conj(input_spec), n=padded_len, axis=0)[:LENGTH]
        filter_grad = filter_grad + filter_term.astype(jnp.float32)
        back_wide = back_grad.astype(jnp.float32)
        key_grad = (back_wide * value_wide).astype(jnp.bfloat16)
        value_grad = (back_wide * key_wide).astype(jnp.bfloat16)
        stacked = jnp.concatenate([key_grad, value_grad], axis=1)
        weight_grad = weight_grad + jnp.dot(tokens[sequence].T, stacked, preferred_element_type=jnp.float32)
    blocks = weight_grad.reshape(ROW_BLOCKS, BLOCK_ROWS, COL_BLOCKS, BLOCK_COLS)
    blocks = blocks.transpose(0, 2, 1, 3).reshape(N_SEQ, BLOCK_ROWS, BLOCK_COLS)
    update = orthogonalize(blocks) * math.sqrt(BLOCK_COLS)
    return (update, filter_grad)
```

```python
import math

import jax
import jax.numpy as jnp
from jax import lax
from jax.sharding import PartitionSpec as P

ROW_BLOCKS = 8
NS_STEPS = 5


COEF_A = 3.4445
COEF_B = -4.775
COEF_C = 2.0315


def fourier_tables(padded_len, outer_len):
    inner_len = padded_len // outer_len
    tables_all = []
    for extent in (outer_len, inner_len):
        grid = (
            lax.broadcasted_iota(jnp.int32, (extent, extent), 0)
            * lax.broadcasted_iota(jnp.int32, (extent, extent), 1)
            % extent
        )
        angle = grid.astype(jnp.float32) * (2.0 * math.pi / extent)
        tables_all.append((jnp.cos(angle), jnp.sin(angle)))
    grid = (
        lax.broadcasted_iota(jnp.int32, (outer_len, inner_len), 0)
        * lax.broadcasted_iota(jnp.int32, (outer_len, inner_len), 1)
        % padded_len
    )
    angle = grid.astype(jnp.float32) * (2.0 * math.pi / padded_len)
    tables_all.append((jnp.cos(angle)[:, :, None], jnp.sin(angle)[:, :, None]))
    return tables_all


def contract(form, left, right):
    return jnp.einsum(form, left, right, precision=lax.Precision.HIGH)


def forward_spectrum(signal, padded_len, tables_all):
    (cosine_outer, sine_outer), (cosine_inner, sine_inner), (twist_cos, twist_sin) = tables_all
    outer_len = cosine_outer.shape[0]
    used_outer = outer_len // 2
    length, chan_count = signal.shape
    cube = signal.reshape(used_outer, padded_len // outer_len, chan_count)
    real_first = contract("an,nmc->amc", cosine_outer[:, :used_outer], cube)
    imag_first = -contract("an,nmc->amc", sine_outer[:, :used_outer], cube)
    real_turn = real_first * twist_cos + imag_first * twist_sin
    imag_turn = imag_first * twist_cos - real_first * twist_sin
    real_spec = contract("amc,mb->abc", real_turn, cosine_inner) + contract(
        "amc,mb->abc", imag_turn, sine_inner
    )
    imag_spec = contract("amc,mb->abc", imag_turn, cosine_inner) - contract(
        "amc,mb->abc", real_turn, sine_inner
    )
    return (real_spec, imag_spec)


def inverse_spectrum(real_spec, imag_spec, padded_len, length, tables_all):
    (cosine_outer, sine_outer), (cosine_inner, sine_inner), (twist_cos, twist_sin) = tables_all
    used_outer = cosine_outer.shape[0] // 2
    real_mid = contract("abc,mb->amc", real_spec, cosine_inner) - contract(
        "abc,mb->amc", imag_spec, sine_inner
    )
    imag_mid = contract("abc,mb->amc", imag_spec, cosine_inner) + contract(
        "abc,mb->amc", real_spec, sine_inner
    )
    real_turn = real_mid * twist_cos - imag_mid * twist_sin
    imag_turn = imag_mid * twist_cos + real_mid * twist_sin
    signal = contract("na,amc->nmc", cosine_outer[:used_outer], real_turn) - contract(
        "na,amc->nmc", sine_outer[:used_outer], imag_turn
    )
    signal = signal / padded_len
    return signal.reshape(length, signal.shape[2])


def replicate_blocks(matrix, row_major, col_major, seq_devs):
    tok_rows = matrix.shape[0]
    block_width = matrix.shape[1] // (row_major if col_major == 1 else col_major)
    pieces = matrix.reshape(tok_rows, matrix.shape[1] // block_width, block_width).transpose(
        1, 0, 2
    )
    if col_major == 1:
        spread = jnp.broadcast_to(
            pieces[:, None], (row_major, seq_devs // row_major, tok_rows, block_width)
        )
    else:
        spread = jnp.broadcast_to(
            pieces[None], (seq_devs // col_major, col_major, tok_rows, block_width)
        )
    return spread.reshape(seq_devs, tok_rows, block_width)


def newton_step(current, gram, last):
    square = jnp.dot(gram, gram, precision=lax.Precision.HIGH)
    mixer = COEF_B * gram + COEF_C * square
    moved = COEF_A * current + jnp.dot(mixer, current, precision=lax.Precision.HIGH)
    if last:
        return moved, None
    half = COEF_A * gram + jnp.dot(mixer, gram, precision=lax.Precision.HIGH)
    following = COEF_A * half + jnp.dot(half, mixer, precision=lax.Precision.HIGH)
    return moved, following


def row_products(current):
    return lax.dot_general(
        current, current, (((1,), (1,)), ((), ())), precision=lax.Precision.HIGHEST
    )


def body(tokens, queries, keys, values, upstream, filters):
    seq_devs = lax.axis_size("seq")
    col_blocks = seq_devs // ROW_BLOCKS
    token_rep = replicate_blocks(tokens[0], ROW_BLOCKS, 1, seq_devs)
    key_wide = keys[0].astype(jnp.float32)
    value_wide = values[0].astype(jnp.float32)
    conv_grad = (upstream[0].astype(jnp.float32) * queries[0].astype(jnp.float32)).astype(
        jnp.bfloat16
    )
    gate_input = (key_wide * value_wide).astype(jnp.bfloat16)
    grad_chan, input_chan = (
        lax.all_to_all(conv_grad, "seq", split_axis=1, concat_axis=0, tiled=True),
        lax.all_to_all(gate_input, "seq", split_axis=1, concat_axis=0, tiled=True),
    )
    length = grad_chan.shape[0]
    padded_len = 2 * length
    outer_len = 2
    while padded_len % (outer_len * 2) == 0 and outer_len * 2 * (outer_len * 2) <= padded_len:
        outer_len = outer_len * 2
    tables_all = fourier_tables(padded_len, outer_len)
    filter_real, filter_imag = forward_spectrum(filters, padded_len, tables_all)
    grad_real, grad_imag = forward_spectrum(grad_chan.astype(jnp.float32), padded_len, tables_all)
    input_real, input_imag = forward_spectrum(
        input_chan.astype(jnp.float32), padded_len, tables_all
    )
    back_chan = inverse_spectrum(
        filter_real * grad_real + filter_imag * grad_imag,
        filter_real * grad_imag - filter_imag * grad_real,
        padded_len,
        length,
        tables_all,
    ).astype(jnp.bfloat16)
    filter_part = inverse_spectrum(
        grad_real * input_real + grad_imag * input_imag,
        grad_imag * input_real - grad_real * input_imag,
        padded_len,
        length,
        tables_all,
    )
    back_tok = lax.all_to_all(back_chan, "seq", split_axis=0, concat_axis=1, tiled=True)
    back_wide = back_tok.astype(jnp.float32)
    stacked = jnp.concatenate(
        [
            (back_wide * value_wide).astype(jnp.bfloat16),
            (back_wide * key_wide).astype(jnp.bfloat16),
        ],
        axis=1,
    )
    grad_rep = replicate_blocks(stacked, ROW_BLOCKS, col_blocks, seq_devs)
    token_blocks, grad_blocks = (
        lax.all_to_all(token_rep, "seq", split_axis=0, concat_axis=1, tiled=True),
        lax.all_to_all(grad_rep, "seq", split_axis=0, concat_axis=1, tiled=True),
    )
    partial_block = lax.dot_general(
        token_blocks[0],
        grad_blocks[0],
        (((0,), (0,)), ((), ())),
        preferred_element_type=jnp.float32,
    )
    filter_grad = lax.psum_scatter(filter_part, "dp", scatter_dimension=0, tiled=True)
    block_cols = partial_block.shape[1]
    half_block = lax.psum_scatter(partial_block, "dp", scatter_dimension=1, tiled=True)
    raw_gram = lax.psum(row_products(half_block), "dp")
    norm = jnp.sqrt(jnp.trace(raw_gram)) + 1e-07
    current = half_block / norm
    gram = raw_gram / (norm * norm)
    for iteration in range(NS_STEPS):
        current, gram = newton_step(current, gram, iteration == NS_STEPS - 1)
    update = current * math.sqrt(block_cols)
    return (update[None], filter_grad)


def solution(mesh):
    return jax.shard_map(
        body,
        mesh=mesh,
        in_specs=(
            P("dp", "seq", None),
            P("dp", "seq", None),
            P("dp", "seq", None),
            P("dp", "seq", None),
            P("dp", "seq", None),
            P(None, "seq"),
        ),
        out_specs=(P("seq", None, "dp"), P("dp", "seq")),
        check_vma=False,
    )
```

```python
import math

import jax
import jax.numpy as jnp
import numpy as np
from jax import lax
from jax.experimental import pallas as pl
from jax.experimental.pallas import tpu as pltpu
from jax.sharding import PartitionSpec as P

F32, BF16 = jnp.float32, jnp.bfloat16
RADIX = 128
HALF = 64
NS_STEPS = 5
COEF_A = 3.4445
COEF_B = -4.775
COEF_C = 2.0315
ROWS = 72


def split_table(table):
    high = np.asarray(table, np.float32).astype(jnp.bfloat16)
    low = (np.asarray(table, np.float64) - high.astype(np.float64)).astype(jnp.bfloat16)
    return high, low


def fourier_tables():
    total = RADIX * RADIX
    spot = np.arange(RADIX)
    used = np.arange(HALF + 1)
    outer = 2.0 * math.pi * (np.outer(used, np.arange(HALF)) % RADIX) / RADIX
    first = np.zeros((2 * ROWS, HALF))
    first[: HALF + 1] = np.cos(outer)
    first[ROWS : ROWS + HALF + 1] = -np.sin(outer)
    weight = np.where((used == 0) | (used == HALF), 1.0, 2.0)[:, None] / total
    last = np.zeros((2 * ROWS, HALF))
    last[: HALF + 1] = np.cos(outer) * weight
    last[ROWS : ROWS + HALF + 1] = -np.sin(outer) * weight
    last = last.T
    inner = 2.0 * math.pi * (np.outer(spot, spot) % RADIX) / RADIX
    real, imag = np.cos(inner), -np.sin(inner)
    forward = np.block([[real, imag], [-imag, real]])
    turn = 2.0 * math.pi * np.outer(used, spot) / total
    twist = np.zeros((2, ROWS, RADIX), np.float32)
    twist[0, : HALF + 1] = np.cos(turn)
    twist[1, : HALF + 1] = -np.sin(turn)
    first_high, first_low = split_table(first)
    last_high, last_low = split_table(last)
    ahead_high, ahead_low = split_table(forward)
    back_high, back_low = split_table(forward.T)
    return (
        np.concatenate([first_high, first_low, first_high], 1),
        np.concatenate([ahead_high, ahead_high, ahead_low], 0),
        np.concatenate([back_high, back_high, back_low], 0),
        np.concatenate([last_high, last_low, last_high], 1),
        twist,
    )


def dot(left, right):
    return jnp.dot(left, right, preferred_element_type=F32)


def parts(value):
    high = value.astype(BF16)
    return high, (value - high.astype(F32)).astype(BF16)


def convolve_pair(grads, inputs, filters, tables):
    first_ref, ahead_ref, back_ref, last_ref, twist_ref = tables
    turn_real, turn_imag = twist_ref[0], twist_ref[1]
    signals = jnp.concatenate([grads[0], inputs[0], grads[1], inputs[1]], axis=1)
    signals = jnp.concatenate([signals, signals], axis=0)
    spread = dot(first_ref[:, : 2 * HALF], signals)
    high, low = parts(jnp.concatenate(filters, axis=1))
    spread_filter = dot(first_ref[...], jnp.concatenate([high, high, low], axis=0))
    turned = []
    for block in (spread, spread_filter):
        for at in range(0, block.shape[1], RADIX):
            real, imag = block[:ROWS, at : at + RADIX], block[ROWS:, at : at + RADIX]
            turned.append(
                jnp.concatenate(
                    [real * turn_real - imag * turn_imag, real * turn_imag + imag * turn_real], axis=1
                )
            )
    high, low = parts(jnp.concatenate(turned, axis=0))
    spectra = dot(jnp.concatenate([high, low, high], axis=1), ahead_ref[...])
    spec = [
        (spectra[i * ROWS : (i + 1) * ROWS, :RADIX], spectra[i * ROWS : (i + 1) * ROWS, RADIX:])
        for i in range(6)
    ]
    products = []
    for which in range(2):
        grad_real, grad_imag = spec[2 * which]
        input_real, input_imag = spec[2 * which + 1]
        filter_real, filter_imag = spec[4 + which]
        for other_real, other_imag, flip in (
            (filter_real, filter_imag, 0),
            (input_real, input_imag, 0),
        ):
            products.append(
                jnp.concatenate(
                    [
                        grad_real * other_real + grad_imag * other_imag,
                        grad_imag * other_real - grad_real * other_imag,
                    ],
                    axis=1,
                )
            )
    high, low = parts(jnp.concatenate(products, axis=0))
    mixed = dot(jnp.concatenate([high, low, high], axis=1), back_ref[...])
    columns = []
    for i in range(4):
        real, imag = mixed[i * ROWS : (i + 1) * ROWS, :RADIX], mixed[i * ROWS : (i + 1) * ROWS, RADIX:]
        columns.append(
            jnp.concatenate(
                [real * turn_real + imag * turn_imag, imag * turn_real - real * turn_imag], axis=0
            )
        )
    high, low = parts(jnp.concatenate(columns, axis=1))
    result = dot(last_ref[...], jnp.concatenate([high, high, low], axis=0))
    return [result[:, i * RADIX : (i + 1) * RADIX] for i in range(4)]


GROUP = 16


def conv_group(at, g_ref, k_ref, v_ref, f_ref, fg_ref, key_rows, value_rows, tables):
    def pair(j, carry):
        chans = [at + 2 * j, at + 2 * j + 1]
        keys = [k_ref[c].astype(F32) for c in chans]
        values = [v_ref[c].astype(F32) for c in chans]
        inputs = [(a * b).astype(BF16) for a, b in zip(keys, values)]
        out = convolve_pair([g_ref[c] for c in chans], inputs, [f_ref[c] for c in chans], tables)
        for i in range(2):
            back = out[2 * i].astype(BF16).astype(F32)
            fg_ref[chans[i]] = out[2 * i + 1]
            key_rows[pl.ds(2 * j + i, HALF, stride=GROUP), :] = back * values[i]
            value_rows[pl.ds(2 * j + i, HALF, stride=GROUP), :] = back * keys[i]
        return carry

    lax.fori_loop(0, GROUP // 2, pair, 0)


def place():
    me = lax.axis_index("seq")
    return me // 32, me // 8 % 4, me // 2 % 4, me % 2


def seq_of(z, x, y, c):
    return ((z * 4 + x) * 4 + y) * 2 + c


def remote(src, dst, send, recv, **device):
    return pltpu.make_async_remote_copy(
        src_ref=src,
        dst_ref=dst,
        send_sem=send,
        recv_sem=recv,
        device_id=device,
        device_id_type=pl.DeviceIdType.MESH,
    )


GROUPS = 4
PIECES = 32


def gradient_kernel(
    g_ref, k_ref, v_ref, f_ref, tok_ref, t0, t1, t2, t3, t4,
    part_ref, fg_ref,
    tok, cols, own, fg_all, fg_in, key_rows, value_rows,
    tok_first, tok_first_send, tok_recv, tok_send, col_recv, col_send, fg_sem,
):
    tables = (t0, t1, t2, t3, t4)
    z, x, y, c = place()
    dp = lax.axis_index("dp")
    up, down, across = (y + 1) % 4, (y + 3) % 4, (y + 2) % 4
    right, left, far = (x + 1) % 4, (x + 3) % 4, (x + 2) % 4
    sibling = seq_of(z, x, y, 1 - c)
    x_right, x_left = seq_of(z, right, y, c), seq_of(z, left, y, c)
    z_other = seq_of(1 - z, x, y, c)

    barrier = pltpu.get_barrier_semaphore()
    friends = [
        seq_of(z, x, up, 0), seq_of(z, x, up, 1), seq_of(z, x, down, 0), seq_of(z, x, down, 1),
        seq_of(z, x, across, c), x_right, x_left, z_other, sibling,
    ]
    for friend in friends:
        pl.semaphore_signal(
            barrier, inc=1, device_id={"seq": friend}, device_id_type=pl.DeviceIdType.MESH
        )
    pl.semaphore_signal(barrier, inc=1, device_id={"dp": 1 - dp}, device_id_type=pl.DeviceIdType.MESH)
    pl.semaphore_wait(barrier, len(friends) + 1)

    pending = []

    def launch(copy):
        copy.start()
        pending.append(copy)

    here = z * 4 + x
    first = []
    for i, target in enumerate((up, down, across)):
        copy = remote(
            tok_ref.at[target], tok.at[here, c, y], tok_first_send.at[i], tok_first.at[i],
            seq=seq_of(z, x, target, c),
        )
        launch(copy)
        first.append(copy)
    local_first = pltpu.make_async_copy(tok_ref.at[y], tok.at[here, c, y], tok_first.at[3])
    local_first.start()

    count = [0]

    def half(zz, xx, cc, h):
        return tok.at[zz * 4 + xx, cc, pl.ds(2 * h, 2)]

    def send_half(zz, xx, h, target):
        launch(
            remote(
                half(zz, xx, c, h), half(zz, xx, c, h), tok_send.at[count[0]],
                tok_recv.at[zz * 4 + xx, c, h], seq=target,
            )
        )
        count[0] += 1

    def wait_half(zz, xx, cc, h):
        pltpu.make_async_copy(
            half(zz, xx, cc, h), half(zz, xx, cc, h), tok_recv.at[zz * 4 + xx, cc, h]
        ).wait()

    def wait_first():
        for i, source in ((0, down), (1, up), (2, across)):
            pltpu.make_async_copy(
                tok.at[here, c, source], tok.at[here, c, source], tok_first.at[i]
            ).wait()
        local_first.wait()

    def spread(zz):
        for a, b in ((0, 1), (1, 0)):
            send_half(zz, x, a, x_right)
            send_half(zz, x, b, x_left)

    def relay(zz):
        wait_half(zz, left, c, 0)
        send_half(zz, left, 0, x_right)
        wait_half(zz, right, c, 1)
        send_half(zz, right, 1, x_left)

    def share(zz, xx, h):
        send_half(zz, xx, h, sibling)

    def slot(yy, cc, i):
        return (yy * 2 + cc) * GROUPS + i

    def send_group(i):
        mine = cols.at[slot(y, c, i)]
        for n, (kind, target) in enumerate(
            ((0, seq_of(z, x, up, 0)), (1, seq_of(z, x, up, 1)), (0, seq_of(z, x, down, 0)), (1, seq_of(z, x, down, 1)))
        ):
            launch(
                remote(own.at[kind, i], mine, col_send.at[i * 5 + n], col_recv.at[slot(y, c, i)], seq=target)
            )
        launch(
            remote(
                own.at[1 - c, i], mine, col_send.at[i * 5 + 4], col_recv.at[slot(y, c, i)], seq=sibling
            )
        )
        pltpu.make_async_copy(own.at[c, i], mine, col_recv.at[slot(y, c, i)]).start()

    def wait_col(at):
        pltpu.make_async_copy(cols.at[at], cols.at[at], col_recv.at[at]).wait()

    forwarded = [0]

    def relay_group(i):
        source, target = (down, up) if i % 2 == 0 else (up, down)
        for cc in range(2):
            at = slot(source, cc, i)
            wait_col(at)
            launch(
                remote(
                    cols.at[at], cols.at[at], col_send.at[5 * GROUPS + forwarded[0]], col_recv.at[at],
                    seq=seq_of(z, x, target, c),
                )
            )
            forwarded[0] += 1

    def compute_group(i):
        conv_group(i * GROUP, g_ref, k_ref, v_ref, f_ref, fg_all, key_rows, value_rows, tables)
        own[0, i] = key_rows[...].reshape(HALF, GROUP, RADIX).astype(BF16)
        own[1, i] = value_rows[...].reshape(HALF, GROUP, RADIX).astype(BF16)

    compute_group(0)
    send_group(0)
    wait_first()
    spread(z)
    for h in range(2):
        send_half(z, x, h, z_other)
        share(z, x, h)
    compute_group(1)
    send_group(1)
    compute_group(2)
    send_group(2)
    relay(z)
    for h in range(2):
        wait_half(1 - z, x, c, h)
    spread(1 - z)
    relay_group(0)
    compute_group(3)
    send_group(3)
    fg_copy = remote(
        fg_all.at[:, pl.ds((1 - dp) * 32, 32)], fg_in, fg_sem.at[0], fg_sem.at[1], dp=1 - dp
    )
    launch(fg_copy)
    relay_group(1)
    for h in range(2):
        share(1 - z, x, h)
    for xx, h in ((left, 0), (right, 1)):
        share(z, xx, h)
    for xx, h in ((left, 1), (right, 0)):
        wait_half(z, xx, c, h)
        share(z, xx, h)
    for h in range(2):
        wait_half(z, far, c, h)
        share(z, far, h)
    relay_group(2)
    relay(1 - z)
    relay_group(3)
    for xx, h in ((left, 0), (right, 1)):
        share(1 - z, xx, h)
    for xx, h in ((left, 1), (right, 0)):
        wait_half(1 - z, xx, c, h)
        share(1 - z, xx, h)
    for h in range(2):
        wait_half(1 - z, far, c, h)
        share(1 - z, far, h)
    fg_copy.wait_recv()
    fg_ref[...] = fg_all[:, pl.ds(dp * 32, 32)] + fg_in[...]
    for i in range(GROUPS):
        wait_col(slot(y, 0, i))
        wait_col(slot(y, 1, i))
        wait_col(slot(across, 0, i))
        wait_col(slot(across, 1, i))
        source = up if i % 2 == 0 else down
        wait_col(slot(source, 0, i))
        wait_col(slot(source, 1, i))

    def multiply(zx, fresh):
        left_side = jnp.concatenate(
            [
                cols[:, zx * 8 + yy * 2 + cc].reshape(PIECES * GROUP, RADIX)
                for cc in range(2)
                for yy in range(4)
            ],
            axis=1,
        )

        def tile(n, carry):
            j, at = n // 2, pl.multiple_of(n % 2 * 256, 256)
            right_side = tok[zx, :, :, :, pl.ds(pl.multiple_of(n * 256, 256), 256)].reshape(1024, 256)
            term = dot(left_side, right_side)
            if fresh:
                part_ref[j, :, pl.ds(at, 256)] = term
            else:
                part_ref[j, :, pl.ds(at, 256)] += term
            return carry

        lax.fori_loop(0, 4, tile, 0)

    for h in range(2):
        wait_half(z, x, 1 - c, h)
    multiply(here, True)

    for zz, xx in ((z, left), (z, right), (z, far), (1 - z, x), (1 - z, left), (1 - z, right), (1 - z, far)):
        for h in range(2):
            wait_half(zz, xx, 1 - c, h)

    def rest(i, carry):
        multiply((here + i) % 8, False)
        return carry

    lax.fori_loop(1, 8, rest, 0)
    for copy in pending:
        copy.wait_send()


def gradient_parts(g, k, v, f, tokens):
    tabs = [jnp.asarray(t) for t in fourier_tables()]
    vm = pl.BlockSpec(memory_space=pltpu.VMEM)
    dma = pltpu.SemaphoreType.DMA
    return pl.pallas_call(
        gradient_kernel,
        out_shape=(
            jax.ShapeDtypeStruct((2, 512, 512), F32),
            jax.ShapeDtypeStruct((64, HALF // 2, RADIX), F32),
        ),
        in_specs=[vm] * 10,
        out_specs=[vm] * 2,
        scratch_shapes=[
            pltpu.VMEM((8, 2, 4, RADIX, 1024), BF16),
            pltpu.VMEM((PIECES, HALF, GROUP, RADIX), BF16),
            pltpu.VMEM((2, GROUPS, HALF, GROUP, RADIX), BF16),
            pltpu.VMEM((64, HALF, RADIX), F32),
            pltpu.VMEM((64, HALF // 2, RADIX), F32),
            pltpu.VMEM((HALF * GROUP, RADIX), F32),
            pltpu.VMEM((HALF * GROUP, RADIX), F32),
            dma((4,)), dma((3,)), dma((8, 2, 2)), dma((32,)), dma((PIECES,)), dma((28,)), dma((2,)),
        ],
        compiler_params=pltpu.CompilerParams(
            collective_id=0, has_side_effects=True, vmem_limit_bytes=56 << 20
        ),
        name="gradient_parts",
    )(g, k, v, f, tokens, *tabs)


def product(left, right):
    left_high, left_low = parts(left)
    right_high, right_low = parts(right)
    left_side = jnp.concatenate([left_high, left_low, left_high], axis=1)
    right_side = jnp.concatenate([right_high, right_high, right_low], axis=0)
    return dot(left_side, right_side)


def newton_kernel(part_ref, update_ref, landed, gram, gram_in, current, send, recv, gram_sem):
    z, x, y, c = place()
    dp = lax.axis_index("dp")
    me = lax.axis_index("seq")
    targets = [
        (seq_of(y // 2, 2 * (y % 2) + j, 2 * c + z, x // 2), x % 2) for j in range(2)
    ]
    source_y, source_c, source_z = 2 * z + x // 2, y // 2, y % 2
    sources = [(seq_of(source_z, 2 * c + dp, source_y, source_c), d) for d in range(2)]
    barrier = pltpu.get_barrier_semaphore()
    expected = jnp.int32(1)
    for seq, d in sources:
        other = jnp.logical_or(seq != me, d != dp)

        @pl.when(other)
        def _():
            pl.semaphore_signal(
                barrier, inc=1, device_id={"seq": seq, "dp": d}, device_id_type=pl.DeviceIdType.MESH
            )

    for seq, d in targets:
        expected = expected + jnp.logical_or(seq != me, d != dp).astype(jnp.int32)
    pl.semaphore_signal(barrier, inc=1, device_id={"dp": 1 - dp}, device_id_type=pl.DeviceIdType.MESH)
    pl.semaphore_wait(barrier, expected)

    for j, (seq, d) in enumerate(targets):
        other = jnp.logical_or(seq != me, d != dp)
        copy = remote(part_ref.at[j], landed.at[dp], send.at[j], recv.at[dp], seq=seq, dp=d)

        @pl.when(other)
        def _():
            copy.start()

        @pl.when(jnp.logical_not(other))
        def _():
            pltpu.make_async_copy(part_ref.at[j], landed.at[dp], recv.at[dp]).start()

    for d in range(2):
        pltpu.make_async_copy(landed.at[d], landed.at[d], recv.at[d]).wait()
    columns = landed[0] + landed[1]
    current[...] = columns.T
    gram[...] = product(current[...], columns)
    exchange = remote(gram, gram_in, gram_sem.at[0], gram_sem.at[1], dp=1 - dp)
    exchange.start()
    exchange.wait()
    raw = gram[...] + gram_in[...]
    diagonal = lax.broadcasted_iota(jnp.int32, raw.shape, 0) == lax.broadcasted_iota(
        jnp.int32, raw.shape, 1
    )
    norm = jnp.sqrt(jnp.sum(jnp.where(diagonal, raw, 0.0), keepdims=True)) + 1e-07
    scale = 1.0 / norm
    gram_in[...] = raw * scale * scale
    current[...] = current[...] * scale

    def step(i, carry):
        gram_now = gram_in[...]
        mixer = COEF_B * gram_now + COEF_C * product(gram_now, gram_now)
        current[...] = COEF_A * current[...] + product(mixer, current[...])
        half = COEF_A * gram_now + product(mixer, gram_now)
        gram_in[...] = COEF_A * half + product(half, mixer)
        return carry

    lax.fori_loop(0, NS_STEPS - 1, step, 0)
    gram_now = gram_in[...]
    mixer = COEF_B * gram_now + COEF_C * product(gram_now, gram_now)
    update_ref[...] = (COEF_A * current[...] + product(mixer, current[...])) * 32.0
    for j, (seq, d) in enumerate(targets):
        other = jnp.logical_or(seq != me, d != dp)
        copy = remote(part_ref.at[j], landed.at[dp], send.at[j], recv.at[dp], seq=seq, dp=d)

        @pl.when(other)
        def _():
            copy.wait_send()


def newton(part):
    vm = pl.BlockSpec(memory_space=pltpu.VMEM)
    dma = pltpu.SemaphoreType.DMA
    return pl.pallas_call(
        newton_kernel,
        out_shape=jax.ShapeDtypeStruct((512, 512), F32),
        in_specs=[vm],
        out_specs=vm,
        scratch_shapes=[
            pltpu.VMEM((2, 512, 512), F32),
            pltpu.VMEM((512, 512), F32),
            pltpu.VMEM((512, 512), F32),
            pltpu.VMEM((512, 512), F32),
            dma((2,)), dma((2,)), dma((2,)),
        ],
        compiler_params=pltpu.CompilerParams(
            collective_id=1, has_side_effects=True, vmem_limit_bytes=48 << 20
        ),
        name="newton",
    )(part)


def quarters(tokens):
    blocks = tokens.reshape(RADIX, 8, 512)
    return jnp.stack([jnp.concatenate([blocks[:, 2 * y], blocks[:, 2 * y + 1]], axis=1) for y in range(4)])


def body(tokens, queries, keys, values, upstream, filters):
    conv_grad = (upstream[0].astype(F32) * queries[0].astype(F32)).astype(BF16)
    sent = jnp.stack([item.T.reshape(64, 64, RADIX) for item in (conv_grad, keys[0], values[0])], axis=1)
    landed = lax.all_to_all(sent, "seq", split_axis=0, concat_axis=0, tiled=True)
    g, k, v = (landed[:, i].transpose(1, 0, 2) for i in range(3))
    f = filters.T.reshape(64, HALF, RADIX)
    part, filter_half = gradient_parts(g, k, v, f, quarters(tokens[0]))
    update = newton(part)
    filter_grad = filter_half.reshape(64, HALF // 2 * RADIX).T
    return (update[None], filter_grad)


def solution(mesh):
    return jax.shard_map(
        body,
        mesh=mesh,
        in_specs=(
            P("dp", "seq", None),
            P("dp", "seq", None),
            P("dp", "seq", None),
            P("dp", "seq", None),
            P("dp", "seq", None),
            P(None, "seq"),
        ),
        out_specs=(P("seq", None, "dp"), P("dp", "seq")),
        check_vma=False,
    )
```

```python
import math

import jax
import jax.numpy as jnp
import numpy as np
from jax import lax
from jax.experimental import pallas as pl
from jax.experimental.pallas import tpu as pltpu
from jax.sharding import PartitionSpec as P

F32, BF16 = jnp.float32, jnp.bfloat16
RADIX = 128
HALF = 64
NS_STEPS = 5
COEF_A = 3.4445
COEF_B = -4.775
COEF_C = 2.0315
ROWS = 72


def split_table(table):
    high = np.asarray(table, np.float32).astype(jnp.bfloat16)
    low = (np.asarray(table, np.float64) - high.astype(np.float64)).astype(jnp.bfloat16)
    return high, low


def fourier_tables():
    total = RADIX * RADIX
    spot = np.arange(RADIX)
    used = np.arange(HALF + 1)
    outer = 2.0 * math.pi * (np.outer(used, np.arange(HALF)) % RADIX) / RADIX
    first = np.zeros((2 * ROWS, HALF))
    first[: HALF + 1] = np.cos(outer)
    first[ROWS : ROWS + HALF + 1] = -np.sin(outer)
    weight = np.where((used == 0) | (used == HALF), 1.0, 2.0)[:, None] / total
    last = np.zeros((2 * ROWS, HALF))
    last[: HALF + 1] = np.cos(outer) * weight
    last[ROWS : ROWS + HALF + 1] = -np.sin(outer) * weight
    last = last.T
    inner = 2.0 * math.pi * (np.outer(spot, spot) % RADIX) / RADIX
    real, imag = np.cos(inner), -np.sin(inner)
    forward = np.block([[real, imag], [-imag, real]])
    turn = 2.0 * math.pi * np.outer(used, spot) / total
    twist = np.zeros((2, ROWS, RADIX), np.float32)
    twist[0, : HALF + 1] = np.cos(turn)
    twist[1, : HALF + 1] = -np.sin(turn)
    first_high, first_low = split_table(first)
    last_high, last_low = split_table(last)
    ahead_high, ahead_low = split_table(forward)
    back_high, back_low = split_table(forward.T)
    return (
        np.concatenate([first_high, first_low, first_high], 1),
        np.concatenate([ahead_high, ahead_high, ahead_low], 0),
        np.concatenate([back_high, back_high, back_low], 0),
        np.concatenate([last_high, last_low, last_high], 1),
        twist,
    )


def dot(left, right):
    return jnp.dot(left, right, preferred_element_type=F32)


def parts(value):
    high = value.astype(BF16)
    return high, (value - high.astype(F32)).astype(BF16)


def convolve_pair(grads, inputs, filters, tables):
    first_ref, ahead_ref, back_ref, last_ref, twist_ref = tables
    turn_real, turn_imag = twist_ref[0], twist_ref[1]
    signals = jnp.concatenate([grads[0], inputs[0], grads[1], inputs[1]], axis=1)
    signals = jnp.concatenate([signals, signals], axis=0)
    spread = dot(first_ref[:, : 2 * HALF], signals)
    high, low = parts(jnp.concatenate(filters, axis=1))
    spread_filter = dot(first_ref[...], jnp.concatenate([high, high, low], axis=0))
    turned = []
    for block in (spread, spread_filter):
        for at in range(0, block.shape[1], RADIX):
            real, imag = block[:ROWS, at : at + RADIX], block[ROWS:, at : at + RADIX]
            turned.append(
                jnp.concatenate(
                    [real * turn_real - imag * turn_imag, real * turn_imag + imag * turn_real], axis=1
                )
            )
    high, low = parts(jnp.concatenate(turned, axis=0))
    spectra = dot(jnp.concatenate([high, low, high], axis=1), ahead_ref[...])
    spec = [
        (spectra[i * ROWS : (i + 1) * ROWS, :RADIX], spectra[i * ROWS : (i + 1) * ROWS, RADIX:])
        for i in range(6)
    ]
    products = []
    for which in range(2):
        grad_real, grad_imag = spec[2 * which]
        input_real, input_imag = spec[2 * which + 1]
        filter_real, filter_imag = spec[4 + which]
        for other_real, other_imag, flip in (
            (filter_real, filter_imag, 0),
            (input_real, input_imag, 0),
        ):
            products.append(
                jnp.concatenate(
                    [
                        grad_real * other_real + grad_imag * other_imag,
                        grad_imag * other_real - grad_real * other_imag,
                    ],
                    axis=1,
                )
            )
    high, low = parts(jnp.concatenate(products, axis=0))
    mixed = dot(jnp.concatenate([high, low, high], axis=1), back_ref[...])
    columns = []
    for i in range(4):
        real, imag = mixed[i * ROWS : (i + 1) * ROWS, :RADIX], mixed[i * ROWS : (i + 1) * ROWS, RADIX:]
        columns.append(
            jnp.concatenate(
                [real * turn_real + imag * turn_imag, imag * turn_real - real * turn_imag], axis=0
            )
        )
    high, low = parts(jnp.concatenate(columns, axis=1))
    result = dot(last_ref[...], jnp.concatenate([high, high, low], axis=0))
    return [result[:, i * RADIX : (i + 1) * RADIX] for i in range(4)]


GROUP = 16


GROUPS = 4


def conv_group(at, in_rows, f_ref, fg_ref, out_rows, tables):
    def pair(j, carry):
        chans = [at + 2 * j, at + 2 * j + 1]
        spots = [pl.ds(2 * j + i, HALF, stride=GROUP) for i in range(2)]
        keys = [in_rows[1, spot, :] for spot in spots]
        values = [in_rows[2, spot, :] for spot in spots]
        inputs = [(a * b).astype(BF16) for a, b in zip(keys, values)]
        grads = [in_rows[0, spot, :].astype(BF16) for spot in spots]
        out = convolve_pair(grads, inputs, [f_ref[chan] for chan in chans], tables)
        for i in range(2):
            back = out[2 * i].astype(BF16).astype(F32)
            fg_ref[chans[i]] = out[2 * i + 1]
            out_rows[0, spots[i], :] = back * values[i]
            out_rows[1, spots[i], :] = back * keys[i]
        return carry

    lax.fori_loop(0, GROUP // 2, pair, 0)


def place():
    me = lax.axis_index("seq")
    return me // 32, me // 8 % 4, me // 2 % 4, me % 2


def seq_of(z, x, y, c):
    return ((z * 4 + x) * 4 + y) * 2 + c


MESH = pl.DeviceIdType.MESH


def remote(src, dst, send, recv, **device):
    return pltpu.make_async_remote_copy(
        src_ref=src, dst_ref=dst, send_sem=send, recv_sem=recv, device_id=device, device_id_type=MESH
    )


def wait_bytes(ref, sem):
    pltpu.make_async_copy(ref, ref, sem).wait()


def product(left, right):
    left_high, left_low = parts(left)
    right_high, right_low = parts(right)
    left_side = jnp.concatenate([left_high, left_low, left_high], axis=1)
    right_side = jnp.concatenate([right_high, right_high, right_low], axis=0)
    return dot(left_side, right_side)


def gradient_kernel(
    sent, f_ref, tok_ref, t0, t1, t2, t3, t4,
    update_ref, fg_ref,
    got, tok, cols, own, fg_all, fg_in, in_rows, out_rows, part, landed, gram, gram_in, current,
    swap_send, swap_recv, swap_own, tok_first, tok_first_send, tok_recv, tok_send, col_recv, col_send,
    fg_sem, part_send, part_recv, gram_send, gram_recv,
):
    tables = (t0, t1, t2, t3, t4)
    z, x, y, c = place()
    me = lax.axis_index("seq")
    dp = lax.axis_index("dp")
    n_seq = lax.axis_size("seq")
    up, down, across = (y + 1) % 4, (y + 3) % 4, (y + 2) % 4
    right, left, far = (x + 1) % 4, (x + 3) % 4, (x + 2) % 4
    sibling = seq_of(z, x, y, 1 - c)
    x_right, x_left = seq_of(z, right, y, c), seq_of(z, left, y, c)
    z_other = seq_of(1 - z, x, y, c)
    targets = [seq_of(j, (y + 2 * j) % 4, 2 * c + z, x // 2) for j in range(2)]
    owner_dp = x % 2
    source = seq_of(y % 2, 2 * c + dp, (x + 2 * z) % 4, y // 2)

    barrier = pltpu.get_barrier_semaphore()

    def greet(d, carry):
        pl.semaphore_signal(barrier, inc=1, device_id={"seq": (me + d) % n_seq}, device_id_type=MESH)
        return carry

    lax.fori_loop(1, n_seq, greet, 0)
    pl.semaphore_signal(barrier, inc=1, device_id={"dp": 1 - dp}, device_id_type=MESH)
    pl.semaphore_signal(barrier, inc=1, device_id={"seq": source, "dp": 1 - dp}, device_id_type=MESH)
    pl.semaphore_wait(barrier, n_seq + 2 * ((x + dp) % 2))

    def swap(d, carry):
        peer = (me + d) % n_seq
        remote(sent.at[peer], got.at[me], swap_send, swap_recv, seq=peer).start()
        return carry

    lax.fori_loop(1, n_seq, swap, 0)
    swap_here = pltpu.make_async_copy(sent.at[me], got.at[me], swap_own)
    swap_here.start()

    pending = []

    def launch(copy):
        copy.start()
        pending.append(copy)

    here = z * 4 + x
    for i, target in enumerate((up, down, across)):
        launch(
            remote(
                tok_ref.at[target], tok.at[here, c, y], tok_first_send.at[i], tok_first.at[i],
                seq=seq_of(z, x, target, c),
            )
        )
    local_first = pltpu.make_async_copy(tok_ref.at[y], tok.at[here, c, y], tok_first.at[3])
    local_first.start()

    count = [0]

    def half(zz, xx, cc, h):
        return tok.at[zz * 4 + xx, cc, pl.ds(2 * h, 2)]

    def send_half(zz, xx, h, target):
        launch(
            remote(
                half(zz, xx, c, h), half(zz, xx, c, h), tok_send.at[count[0]],
                tok_recv.at[zz * 4 + xx, c, h], seq=target,
            )
        )
        count[0] += 1

    def wait_half(zz, xx, cc, h):
        wait_bytes(half(zz, xx, cc, h), tok_recv.at[zz * 4 + xx, cc, h])

    def wait_first():
        for i, source_y in ((0, down), (1, up), (2, across)):
            wait_bytes(tok.at[here, c, source_y], tok_first.at[i])
        local_first.wait()

    def spread(zz):
        for a, b in ((0, 1), (1, 0)):
            send_half(zz, x, a, x_right)
            send_half(zz, x, b, x_left)

    def relay(zz):
        wait_half(zz, left, c, 0)
        send_half(zz, left, 0, x_right)
        wait_half(zz, right, c, 1)
        send_half(zz, right, 1, x_left)

    def share(zz, xx, h):
        send_half(zz, xx, h, sibling)

    def slot(yy, cc, i):
        return (yy * 2 + cc, i)

    def send_group(i):
        mine = cols.at[slot(y, c, i)]
        arrival = col_recv.at[slot(y, c, i)]
        for n, (kind, target) in enumerate(((0, up), (1, up), (0, down), (1, down))):
            launch(
                remote(own.at[kind, i], mine, col_send.at[i * 5 + n], arrival, seq=seq_of(z, x, target, kind))
            )
        launch(remote(own.at[1 - c, i], mine, col_send.at[i * 5 + 4], arrival, seq=sibling))
        pltpu.make_async_copy(own.at[c, i], mine, arrival).start()

    def wait_col(at):
        wait_bytes(cols.at[at], col_recv.at[at])

    forwarded = [0]

    def relay_group(i):
        source_y, target = (down, up) if i % 2 == 0 else (up, down)
        for cc in range(2):
            at = slot(source_y, cc, i)
            wait_col(at)
            launch(
                remote(
                    cols.at[at], cols.at[at], col_send.at[5 * GROUPS + forwarded[0]], col_recv.at[at],
                    seq=seq_of(z, x, target, c),
                )
            )
            forwarded[0] += 1

    def compute_group(i):
        for kind in range(3):
            in_rows[kind] = got[:, kind, GROUP * i : GROUP * (i + 1), :].astype(F32).reshape(HALF * GROUP, RADIX)
        conv_group(i * GROUP, in_rows, f_ref, fg_all, out_rows, tables)
        for kind in range(2):
            own[kind, i] = out_rows[kind].reshape(HALF, GROUP, RADIX).astype(BF16)

    wait_bytes(got.at[pl.ds(0, 63)], swap_recv)
    swap_here.wait()
    wait_first()
    spread(z)
    for h in range(2):
        send_half(z, x, h, z_other)
        share(z, x, h)
    compute_group(0)
    send_group(0)
    relay(z)
    compute_group(1)
    send_group(1)
    for h in range(2):
        wait_half(1 - z, x, c, h)
    spread(1 - z)
    relay_group(0)
    for xx, h in ((left, 0), (right, 1)):
        share(z, xx, h)
    compute_group(2)
    send_group(2)
    relay_group(1)
    for h in range(2):
        share(1 - z, x, h)
    compute_group(3)
    send_group(3)
    fg_copy = remote(
        fg_all.at[:, pl.ds((1 - dp) * 32, 32)], fg_in, fg_sem.at[0], fg_sem.at[1], dp=1 - dp
    )
    launch(fg_copy)
    relay(1 - z)
    relay_group(2)
    for xx, h in ((left, 1), (right, 0)):
        wait_half(z, xx, c, h)
        share(z, xx, h)
    for h in range(2):
        wait_half(z, far, c, h)
        share(z, far, h)
    for xx, h in ((left, 0), (right, 1)):
        share(1 - z, xx, h)
    for xx, h in ((left, 1), (right, 0)):
        wait_half(1 - z, xx, c, h)
        share(1 - z, xx, h)
    relay_group(3)
    for h in range(2):
        wait_half(1 - z, far, c, h)
        share(1 - z, far, h)

    def wait_group(i):
        for cc in range(2):
            wait_col(slot(y, cc, i))
            wait_col(slot(across, cc, i))
            wait_col(slot(up if i % 2 == 0 else down, cc, i))

    def multiply(zx, side, fresh):
        left_side = jnp.concatenate(
            [
                cols[:, pl.ds(2 * side, 2), zx * 8 + yy * 2 + cc].reshape(256, RADIX)
                for cc in range(2)
                for yy in range(4)
            ],
            axis=1,
        )

        def tile(n, carry):
            j, at = n // 2, pl.multiple_of(n % 2 * 256, 256)
            right_side = tok[zx, :, :, :, pl.ds(pl.multiple_of(n * 256, 256), 256)].reshape(1024, 256)
            term = dot(left_side, right_side).reshape(8, 32, 256)
            if fresh:
                part[j, :, pl.ds(32 * side, 32), pl.ds(at, 256)] = term
            else:
                part[j, :, pl.ds(32 * side, 32), pl.ds(at, 256)] += term
            return carry

        lax.fori_loop(0, 4, tile, 0)

    stays = [jnp.logical_and(target == me, owner_dp == dp) for target in targets]

    def part_copy(j, side):
        view = (slice(None), pl.ds(32 * side, 32))
        src, dst = part.at[(j, *view)], landed.at[(dp, *view)]
        arrival = part_recv.at[dp, side]
        away = remote(src, dst, part_send.at[j, side], arrival, seq=targets[j], dp=owner_dp)
        return away, pltpu.make_async_copy(src, dst, arrival)

    def send_parts(side):
        for j in range(2):
            away, at_home = part_copy(j, side)

            @pl.when(stays[j])
            def _():
                at_home.start()

            @pl.when(jnp.logical_not(stays[j]))
            def _():
                away.start()

    def rest(side):
        def more(i, carry):
            multiply((here + i) % 8, side, False)
            return carry

        lax.fori_loop(1, 8, more, 0)

    for i in (0, 1):
        wait_group(i)
    for h in range(2):
        wait_half(z, x, 1 - c, h)
    multiply(here, 0, True)
    for zz, xx in ((z, left), (z, right), (z, far), (1 - z, x), (1 - z, left), (1 - z, right), (1 - z, far)):
        for h in range(2):
            wait_half(zz, xx, 1 - c, h)
    rest(0)
    send_parts(0)
    for i in (2, 3):
        wait_group(i)
    multiply(here, 1, True)
    rest(1)
    send_parts(1)
    fg_copy.wait_recv()
    fg_ref[...] = fg_all[:, pl.ds(dp * 32, 32)] + fg_in[...]

    for side in range(2):
        view = (slice(None), pl.ds(32 * side, 32))
        for d in range(2):
            wait_bytes(landed.at[(d, *view)], part_recv.at[d, side])
        columns = (landed[0, :, pl.ds(32 * side, 32), :] + landed[1, :, pl.ds(32 * side, 32), :]).reshape(256, 512)
        term = product(columns.T, columns)
        if side == 0:
            gram[...] = term
        else:
            gram[...] += term
    exchanges = []
    for i in range(4):
        view = (pl.ds(128 * i, 128), pl.ds(128 * i, 512 - 128 * i))
        copy = remote(gram.at[view], gram_in.at[view], gram_send.at[i], gram_recv.at[i], dp=1 - dp)
        launch(copy)
        exchanges.append(copy)
    current[...] = (landed[0] + landed[1]).reshape(512, 512).T
    for copy in exchanges:
        copy.wait_recv()
    diagonal = lax.broadcasted_iota(jnp.int32, (128, 128), 0) == lax.broadcasted_iota(jnp.int32, (128, 128), 1)
    trace = jnp.zeros((1, 1), F32)
    for i in range(4):
        block = gram[128 * i : 128 * (i + 1), 128 * i : 128 * (i + 1)]
        block = block + gram_in[128 * i : 128 * (i + 1), 128 * i : 128 * (i + 1)]
        trace = trace + jnp.sum(jnp.where(diagonal, block, 0.0), keepdims=True)
    scale = 1.0 / (jnp.sqrt(trace) + 1e-07)
    for i in range(4):
        for j in range(i, 4):
            at = (slice(128 * i, 128 * (i + 1)), slice(128 * j, 128 * (j + 1)))
            block = (gram[at] + gram_in[at]) * scale * scale
            gram_in[at] = block
            if j > i:
                gram_in[at[1], at[0]] = block.T
    current[...] = current[...] * scale

    def step(i, carry):
        gram_now = gram_in[...]
        mixer = COEF_B * gram_now + COEF_C * product(gram_now, gram_now)
        current[...] = COEF_A * current[...] + product(mixer, current[...])
        half_step = COEF_A * gram_now + product(mixer, gram_now)
        gram_in[...] = COEF_A * half_step + product(half_step, mixer)
        return carry

    lax.fori_loop(0, NS_STEPS - 1, step, 0)
    gram_now = gram_in[...]
    mixer = COEF_B * gram_now + COEF_C * product(gram_now, gram_now)
    update_ref[...] = (COEF_A * current[...] + product(mixer, current[...])) * 32.0

    for side in range(2):
        for j in range(2):
            away, _ = part_copy(j, side)

            @pl.when(jnp.logical_not(stays[j]))
            def _():
                away.wait_send()

    wait_bytes(sent.at[pl.ds(0, 63)], swap_send)
    for copy in pending:
        copy.wait_send()


def gradients(sent, f, tokens):
    tabs = [jnp.asarray(t) for t in fourier_tables()]
    vm = pl.BlockSpec(memory_space=pltpu.VMEM)
    dma = pltpu.SemaphoreType.DMA
    square = pltpu.VMEM((512, 512), F32)
    return pl.pallas_call(
        gradient_kernel,
        out_shape=(
            jax.ShapeDtypeStruct((512, 512), F32),
            jax.ShapeDtypeStruct((64, HALF // 2, RADIX), F32),
        ),
        in_specs=[vm] * 8,
        out_specs=[vm] * 2,
        scratch_shapes=[
            pltpu.VMEM((64, 3, 64, RADIX), BF16),
            pltpu.VMEM((8, 2, 4, RADIX, 1024), BF16),
            pltpu.VMEM((8, GROUPS, HALF, GROUP, RADIX), BF16),
            pltpu.VMEM((2, GROUPS, HALF, GROUP, RADIX), BF16),
            pltpu.VMEM((64, HALF, RADIX), F32),
            pltpu.VMEM((64, HALF // 2, RADIX), F32),
            pltpu.VMEM((3, HALF * GROUP, RADIX), F32),
            pltpu.VMEM((2, HALF * GROUP, RADIX), F32),
            pltpu.VMEM((2, 8, 64, 512), F32),
            pltpu.VMEM((2, 8, 64, 512), F32),
            square, square, square,
            dma, dma, dma, dma((4,)), dma((3,)), dma((8, 2, 2)), dma((32,)), dma((8, GROUPS)), dma((28,)),
            dma((2,)), dma((2, 2)), dma((2, 2)), dma((4,)), dma((4,)),
        ],
        compiler_params=pltpu.CompilerParams(
            collective_id=0, has_side_effects=True, vmem_limit_bytes=60 << 20
        ),
        name="gradients",
    )(sent, f, tokens, *tabs)


def quarters(tokens):
    blocks = tokens.reshape(RADIX, 8, 512)
    return jnp.stack(
        [jnp.concatenate([blocks[:, y], blocks[:, 4 + (y + 2) % 4]], axis=1) for y in range(4)]
    )


def body(tokens, queries, keys, values, upstream, filters):
    conv_grad = (upstream[0].astype(F32) * queries[0].astype(F32)).astype(BF16)
    sent = jnp.stack([item.T.reshape(64, 64, RADIX) for item in (conv_grad, keys[0], values[0])], axis=1)
    f = filters.T.reshape(64, HALF, RADIX)
    update, filter_half = gradients(sent, f, quarters(tokens[0]))
    filter_grad = filter_half.reshape(64, HALF // 2 * RADIX).T
    return (update[None], filter_grad)


def solution(mesh):
    return jax.shard_map(
        body,
        mesh=mesh,
        in_specs=(
            P("dp", "seq", None),
            P("dp", "seq", None),
            P("dp", "seq", None),
            P("dp", "seq", None),
            P("dp", "seq", None),
            P(None, "seq"),
        ),
        out_specs=(P("seq", None, "dp"), P("dp", "seq")),
        check_vma=False,
    )
```

```python
import math

import jax
import jax.numpy as jnp
import numpy as np
from jax import lax
from jax.experimental import pallas as pl
from jax.experimental.pallas import tpu as pltpu
from jax.sharding import PartitionSpec as P

F32, BF16 = jnp.float32, jnp.bfloat16
RADIX = 128
HALF = 64
NS_STEPS = 5
COEF_A = 3.4445
COEF_B = -4.775
COEF_C = 2.0315
ROWS = 72


def split_table(table):
    high = np.asarray(table, np.float32).astype(jnp.bfloat16)
    low = (np.asarray(table, np.float64) - high.astype(np.float64)).astype(jnp.bfloat16)
    return high, low


def fourier_tables():
    total = RADIX * RADIX
    spot = np.arange(RADIX)
    used = np.arange(HALF + 1)
    outer = 2.0 * math.pi * (np.outer(used, np.arange(HALF)) % RADIX) / RADIX
    first = np.zeros((2 * ROWS, HALF))
    first[: HALF + 1] = np.cos(outer)
    first[ROWS : ROWS + HALF + 1] = -np.sin(outer)
    weight = np.where((used == 0) | (used == HALF), 1.0, 2.0)[:, None] / total
    last = np.zeros((2 * ROWS, HALF))
    last[: HALF + 1] = np.cos(outer) * weight
    last[ROWS : ROWS + HALF + 1] = -np.sin(outer) * weight
    last = last.T
    inner = 2.0 * math.pi * (np.outer(spot, spot) % RADIX) / RADIX
    real, imag = np.cos(inner), -np.sin(inner)
    forward = np.block([[real, imag], [-imag, real]])
    turn = 2.0 * math.pi * np.outer(used, spot) / total
    twist = np.zeros((2, ROWS, RADIX), np.float32)
    twist[0, : HALF + 1] = np.cos(turn)
    twist[1, : HALF + 1] = -np.sin(turn)
    first_high, first_low = split_table(first)
    last_high, last_low = split_table(last)
    ahead_high, ahead_low = split_table(forward)
    back_high, back_low = split_table(forward.T)
    return (
        np.concatenate([first_high, first_low, first_high], 1),
        np.concatenate([ahead_high, ahead_high, ahead_low], 0),
        np.concatenate([back_high, back_high, back_low], 0),
        np.concatenate([last_high, last_low, last_high], 1),
        twist,
    )


def dot(left, right):
    return jnp.dot(left, right, preferred_element_type=F32)


def parts(value):
    high = value.astype(BF16)
    return high, (value - high.astype(F32)).astype(BF16)


def convolve_pair(grads, inputs, filters, tables):
    first_ref, ahead_ref, back_ref, last_ref, twist_ref = tables
    turn_real, turn_imag = twist_ref[0], twist_ref[1]
    signals = jnp.concatenate([grads[0], inputs[0], grads[1], inputs[1]], axis=1)
    signals = jnp.concatenate([signals, signals], axis=0)
    spread = dot(first_ref[:, : 2 * HALF], signals)
    high, low = parts(jnp.concatenate(filters, axis=1))
    spread_filter = dot(first_ref[...], jnp.concatenate([high, high, low], axis=0))
    turned = []
    for block in (spread, spread_filter):
        for at in range(0, block.shape[1], RADIX):
            real, imag = block[:ROWS, at : at + RADIX], block[ROWS:, at : at + RADIX]
            turned.append(
                jnp.concatenate(
                    [real * turn_real - imag * turn_imag, real * turn_imag + imag * turn_real], axis=1
                )
            )
    high, low = parts(jnp.concatenate(turned, axis=0))
    spectra = dot(jnp.concatenate([high, low, high], axis=1), ahead_ref[...])
    spec = [
        (spectra[i * ROWS : (i + 1) * ROWS, :RADIX], spectra[i * ROWS : (i + 1) * ROWS, RADIX:])
        for i in range(6)
    ]
    products = []
    for which in range(2):
        grad_real, grad_imag = spec[2 * which]
        input_real, input_imag = spec[2 * which + 1]
        filter_real, filter_imag = spec[4 + which]
        for other_real, other_imag, flip in (
            (filter_real, filter_imag, 0),
            (input_real, input_imag, 0),
        ):
            products.append(
                jnp.concatenate(
                    [
                        grad_real * other_real + grad_imag * other_imag,
                        grad_imag * other_real - grad_real * other_imag,
                    ],
                    axis=1,
                )
            )
    high, low = parts(jnp.concatenate(products, axis=0))
    mixed = dot(jnp.concatenate([high, low, high], axis=1), back_ref[...])
    columns = []
    for i in range(4):
        real, imag = mixed[i * ROWS : (i + 1) * ROWS, :RADIX], mixed[i * ROWS : (i + 1) * ROWS, RADIX:]
        columns.append(
            jnp.concatenate(
                [real * turn_real + imag * turn_imag, imag * turn_real - real * turn_imag], axis=0
            )
        )
    high, low = parts(jnp.concatenate(columns, axis=1))
    result = dot(last_ref[...], jnp.concatenate([high, high, low], axis=0))
    return [result[:, i * RADIX : (i + 1) * RADIX] for i in range(4)]


GROUP = 16


GROUPS = 4


def conv_group(at, in_rows, f_ref, fg_ref, out_rows, tables):
    def pair(j, carry):
        chans = [at + 2 * j, at + 2 * j + 1]
        spots = [pl.ds(2 * j + i, HALF, stride=GROUP) for i in range(2)]
        keys = [in_rows[1, spot, :] for spot in spots]
        values = [in_rows[2, spot, :] for spot in spots]
        inputs = [(a * b).astype(BF16) for a, b in zip(keys, values)]
        grads = [in_rows[0, spot, :].astype(BF16) for spot in spots]
        out = convolve_pair(grads, inputs, [f_ref[chan] for chan in chans], tables)
        for i in range(2):
            back = out[2 * i].astype(BF16).astype(F32)
            fg_ref[chans[i]] = out[2 * i + 1]
            out_rows[0, spots[i], :] = back * values[i]
            out_rows[1, spots[i], :] = back * keys[i]
        return carry

    lax.fori_loop(0, GROUP // 2, pair, 0)


STRIDE = 37


def place():
    me = lax.axis_index("seq")
    return me // 32, me // 8 % 4, me // 2 % 4, me % 2


def seq_of(z, x, y, c):
    return ((z * 4 + x) * 4 + y) * 2 + c


MESH = pl.DeviceIdType.MESH


def remote(src, dst, send, recv, **device):
    return pltpu.make_async_remote_copy(
        src_ref=src, dst_ref=dst, send_sem=send, recv_sem=recv, device_id=device, device_id_type=MESH
    )


def wait_bytes(ref, sem):
    pltpu.make_async_copy(ref, ref, sem).wait()


def product(left, right):
    left_high, left_low = parts(left)
    right_high, right_low = parts(right)
    left_side = jnp.concatenate([left_high, left_low, left_high], axis=1)
    right_side = jnp.concatenate([right_high, right_high, right_low], axis=0)
    return dot(left_side, right_side)


def gradient_kernel(
    sent, f_ref, tok_ref, t0, t1, t2, t3, t4,
    update_ref, fg_ref,
    got, tok, cols, own, fg_all, fg_in, in_rows, out_rows, part, landed, gram, gram_in, current,
    swap_send, swap_recv, swap_own, tok_first, tok_first_send, tok_recv, tok_send, col_recv, col_send,
    fg_sem, part_send, part_recv, gram_send, gram_recv, final_sem,
):
    tables = (t0, t1, t2, t3, t4)
    z, x, y, c = place()
    me = lax.axis_index("seq")
    dp = lax.axis_index("dp")
    n_seq = lax.axis_size("seq")
    up, down, across = (y + 1) % 4, (y + 3) % 4, (y + 2) % 4
    right, left, far = (x + 1) % 4, (x + 3) % 4, (x + 2) % 4
    sibling = seq_of(z, x, y, 1 - c)
    x_right, x_left = seq_of(z, right, y, c), seq_of(z, left, y, c)
    z_other = seq_of(1 - z, x, y, c)
    mine = (dp + c + x // 2) % 2
    mate = seq_of(z, x + 1 - 2 * (x % 2), y, c)
    owner = seq_of(y // 2, 2 * (y % 2) + mine, 2 * c + z, x // 2)
    owner_dp = x % 2
    source = seq_of(y % 2, 2 * c + dp, 2 * z + x // 2, y // 2)
    source_dp = (x + y // 2 + c) % 2

    barrier = pltpu.get_barrier_semaphore()

    def greet(d, carry):
        pl.semaphore_signal(barrier, inc=1, device_id={"seq": (me + d) % n_seq}, device_id_type=MESH)
        return carry

    lax.fori_loop(1, n_seq, greet, 0)
    pl.semaphore_signal(barrier, inc=1, device_id={"dp": 1 - dp}, device_id_type=MESH)

    @pl.when(source_dp != dp)
    def _():
        pl.semaphore_signal(barrier, inc=1, device_id={"seq": source, "dp": 1 - dp}, device_id_type=MESH)

    pl.semaphore_wait(barrier, n_seq + (owner_dp + dp) % 2)

    def swap(part_at):
        def one(d, carry):
            peer = (me + STRIDE * d) % n_seq
            remote(
                sent.at[peer, part_at], got.at[part_at, me], swap_send.at[part_at], swap_recv.at[part_at], seq=peer
            ).start()
            return carry

        lax.fori_loop(1, n_seq, one, 0)
        pltpu.make_async_copy(sent.at[me, part_at], got.at[part_at, me], swap_own.at[part_at]).start()

    def wait_swap(part_at):
        wait_bytes(got.at[part_at, pl.ds(0, 63)], swap_recv.at[part_at])
        wait_bytes(got.at[part_at, 0], swap_own.at[part_at])

    swap(0)

    pending = []

    def launch(copy):
        copy.start()
        pending.append(copy)

    here = z * 4 + x

    def quarter(at):
        return tok_ref.at[:, pl.ds(pl.multiple_of(at * 1024, 1024), 1024)]

    for i, target in enumerate((up, down, across)):
        launch(
            remote(
                quarter(target), tok.at[here, c, y], tok_first_send.at[i], tok_first.at[i],
                seq=seq_of(z, x, target, c),
            )
        )
    local_first = pltpu.make_async_copy(quarter(y), tok.at[here, c, y], tok_first.at[3])
    local_first.start()
    swap(1)

    count = [0]

    def half(zz, xx, cc, h):
        return tok.at[zz * 4 + xx, cc, pl.ds(2 * h, 2)]

    def send_half(zz, xx, h, target):
        launch(
            remote(
                half(zz, xx, c, h), half(zz, xx, c, h), tok_send.at[count[0]],
                tok_recv.at[zz * 4 + xx, c, h], seq=target,
            )
        )
        count[0] += 1

    def wait_half(zz, xx, cc, h):
        wait_bytes(half(zz, xx, cc, h), tok_recv.at[zz * 4 + xx, cc, h])

    def wait_first():
        for i, source_y in ((0, down), (1, up), (2, across)):
            wait_bytes(tok.at[here, c, source_y], tok_first.at[i])
        local_first.wait()

    def spread(zz):
        for a, b in ((0, 1), (1, 0)):
            send_half(zz, x, a, x_right)
            send_half(zz, x, b, x_left)

    def relay(zz):
        wait_half(zz, left, c, 0)
        send_half(zz, left, 0, x_right)
        wait_half(zz, right, c, 1)
        send_half(zz, right, 1, x_left)

    def share(zz, xx, h):
        send_half(zz, xx, h, sibling)

    def slot(yy, cc, i):
        return (yy * 2 + cc, i)

    def send_group(i):
        mine = cols.at[slot(y, c, i)]
        arrival = col_recv.at[slot(y, c, i)]
        for n, (kind, target) in enumerate(((0, up), (1, up), (0, down), (1, down))):
            launch(
                remote(own.at[kind, i], mine, col_send.at[i * 5 + n], arrival, seq=seq_of(z, x, target, kind))
            )
        launch(remote(own.at[1 - c, i], mine, col_send.at[i * 5 + 4], arrival, seq=sibling))
        pltpu.make_async_copy(own.at[c, i], mine, arrival).start()

    def wait_col(at):
        wait_bytes(cols.at[at], col_recv.at[at])

    forwarded = [0]

    def relay_group(i):
        source_y, target = (down, up) if i % 2 == 0 else (up, down)
        for cc in range(2):
            at = slot(source_y, cc, i)
            wait_col(at)
            launch(
                remote(
                    cols.at[at], cols.at[at], col_send.at[5 * GROUPS + forwarded[0]], col_recv.at[at],
                    seq=seq_of(z, x, target, c),
                )
            )
            forwarded[0] += 1

    def compute_group(i):
        for kind in range(3):
            in_rows[kind] = got[i // 2, :, kind, pl.ds(GROUP * (i % 2), GROUP), :].astype(F32).reshape(HALF * GROUP, RADIX)
        conv_group(i * GROUP, in_rows, f_ref, fg_all, out_rows, tables)
        for kind in range(2):
            own[kind, i] = out_rows[kind].reshape(HALF, GROUP, RADIX).astype(BF16)

    wait_swap(0)
    compute_group(0)
    send_group(0)
    wait_first()
    spread(z)
    for h in range(2):
        send_half(z, x, h, z_other)
        share(z, x, h)
    compute_group(1)
    send_group(1)
    relay(z)
    relay_group(0)
    for xx, h in ((left, 0), (right, 1)):
        share(z, xx, h)
    wait_swap(1)
    compute_group(2)
    send_group(2)
    for h in range(2):
        wait_half(1 - z, x, c, h)
    spread(1 - z)
    relay_group(1)
    for h in range(2):
        share(1 - z, x, h)
    compute_group(3)
    send_group(3)
    fg_copy = remote(
        fg_all.at[:, pl.ds((1 - dp) * 32, 32)], fg_in, fg_sem.at[0], fg_sem.at[1], dp=1 - dp
    )
    launch(fg_copy)
    relay(1 - z)
    relay_group(2)
    for xx, h in ((left, 1), (right, 0)):
        wait_half(z, xx, c, h)
        share(z, xx, h)
    for h in range(2):
        wait_half(z, far, c, h)
        share(z, far, h)
    for xx, h in ((left, 0), (right, 1)):
        share(1 - z, xx, h)
    for xx, h in ((left, 1), (right, 0)):
        wait_half(1 - z, xx, c, h)
        share(1 - z, xx, h)
    relay_group(3)
    for h in range(2):
        wait_half(1 - z, far, c, h)
        share(1 - z, far, h)

    def wait_group(i):
        for cc in range(2):
            wait_col(slot(y, cc, i))
            wait_col(slot(across, cc, i))
            wait_col(slot(up if i % 2 == 0 else down, cc, i))

    def multiply(zx, side, fresh):
        left_side = jnp.concatenate(
            [
                cols[:, pl.ds(2 * side, 2), zx * 8 + yy * 2 + cc].reshape(256, RADIX)
                for cc in range(2)
                for yy in range(4)
            ],
            axis=1,
        )

        def tile(n, carry):
            j, at = n // 2, pl.multiple_of(n % 2 * 256, 256)
            right_side = tok[zx, :, :, :, pl.ds(pl.multiple_of(n * 256, 256), 256)].reshape(1024, 256)
            term = dot(left_side, right_side).reshape(8, 32, 256)
            if fresh:
                part[j, :, pl.ds(32 * side, 32), pl.ds(at, 256)] = term
            else:
                part[j, :, pl.ds(32 * side, 32), pl.ds(at, 256)] += term
            return carry

        lax.fori_loop(0, 4, tile, 0)

    def sum_copy(side):
        return remote(
            part.at[1 - mine, :, pl.ds(32 * side, 32)], landed.at[:, pl.ds(32 * side, 32)],
            part_send.at[side], part_recv.at[side], dp=1 - dp,
        )

    def rest(side):
        def more(i, carry):
            multiply((here + i) % 8, side, False)
            return carry

        lax.fori_loop(1, 8, more, 0)

    for i in (0, 1):
        wait_group(i)
    for h in range(2):
        wait_half(z, x, 1 - c, h)
    multiply(here, 0, True)
    for zz, xx in ((z, left), (z, right), (z, far), (1 - z, x), (1 - z, left), (1 - z, right), (1 - z, far)):
        for h in range(2):
            wait_half(zz, xx, 1 - c, h)
    rest(0)
    launch(sum_copy(0))
    for i in (2, 3):
        wait_group(i)
    multiply(here, 1, True)
    rest(1)
    launch(sum_copy(1))
    fg_copy.wait_recv()
    fg_ref[...] = fg_all[:, pl.ds(dp * 32, 32)] + fg_in[...]

    for side in range(2):
        sum_copy(side).wait_recv()
        columns = part[mine, :, pl.ds(32 * side, 32), :] + landed[:, pl.ds(32 * side, 32), :]
        landed[:, pl.ds(32 * side, 32), :] = columns
        columns = columns.reshape(256, 512)
        term = product(columns.T, columns)
        if side == 0:
            gram[...] = term
        else:
            gram[...] += term
    exchanges = []
    for i in range(4):
        view = (pl.ds(128 * i, 128), pl.ds(128 * i, 512 - 128 * i))
        copy = remote(gram.at[view], gram_in.at[view], gram_send.at[i], gram_recv.at[i], seq=mate)
        launch(copy)
        exchanges.append(copy)
    current[...] = landed[...].reshape(512, 512).T
    for copy in exchanges:
        copy.wait_recv()
    diagonal = lax.broadcasted_iota(jnp.int32, (128, 128), 0) == lax.broadcasted_iota(jnp.int32, (128, 128), 1)
    trace = jnp.zeros((1, 1), F32)
    for i in range(4):
        block = gram[128 * i : 128 * (i + 1), 128 * i : 128 * (i + 1)]
        block = block + gram_in[128 * i : 128 * (i + 1), 128 * i : 128 * (i + 1)]
        trace = trace + jnp.sum(jnp.where(diagonal, block, 0.0), keepdims=True)
    scale = 1.0 / (jnp.sqrt(trace) + 1e-07)
    for i in range(4):
        for j in range(i, 4):
            at = (slice(128 * i, 128 * (i + 1)), slice(128 * j, 128 * (j + 1)))
            block = (gram[at] + gram_in[at]) * scale * scale
            gram_in[at] = block
            if j > i:
                gram_in[at[1], at[0]] = block.T
    current[...] = current[...] * scale

    def step(i, carry):
        gram_now = gram_in[...]
        mixer = COEF_B * gram_now + COEF_C * product(gram_now, gram_now)
        current[...] = COEF_A * current[...] + product(mixer, current[...])
        half_step = COEF_A * gram_now + product(mixer, gram_now)
        gram_in[...] = COEF_A * half_step + product(half_step, mixer)
        return carry

    lax.fori_loop(0, NS_STEPS - 1, step, 0)
    gram_now = gram_in[...]
    mixer = COEF_B * gram_now + COEF_C * product(gram_now, gram_now)
    current[...] = (COEF_A * current[...] + product(mixer, current[...])) * 32.0
    stays = jnp.logical_and(owner == me, owner_dp == dp)
    away = remote(current, update_ref, final_sem.at[0], final_sem.at[1], seq=owner, dp=owner_dp)

    @pl.when(stays)
    def _():
        pltpu.make_async_copy(current, update_ref, final_sem.at[1]).start()

    @pl.when(jnp.logical_not(stays))
    def _():
        away.start()

    wait_bytes(update_ref, final_sem.at[1])

    @pl.when(jnp.logical_not(stays))
    def _():
        away.wait_send()

    for i in range(2):
        wait_bytes(got.at[i, pl.ds(0, 63)], swap_send.at[i])
    for copy in pending:
        copy.wait_send()


def gradients(sent, f, tokens):
    tabs = [jnp.asarray(t) for t in fourier_tables()]
    vm = pl.BlockSpec(memory_space=pltpu.VMEM)
    dma = pltpu.SemaphoreType.DMA
    square = pltpu.VMEM((512, 512), F32)
    return pl.pallas_call(
        gradient_kernel,
        out_shape=(
            jax.ShapeDtypeStruct((512, 512), F32),
            jax.ShapeDtypeStruct((64, HALF // 2, RADIX), F32),
        ),
        in_specs=[vm] * 8,
        out_specs=[vm] * 2,
        scratch_shapes=[
            pltpu.VMEM((2, 64, 3, 32, RADIX), BF16),
            pltpu.VMEM((8, 2, 4, RADIX, 1024), BF16),
            pltpu.VMEM((8, GROUPS, HALF, GROUP, RADIX), BF16),
            pltpu.VMEM((2, GROUPS, HALF, GROUP, RADIX), BF16),
            pltpu.VMEM((64, HALF, RADIX), F32),
            pltpu.VMEM((64, HALF // 2, RADIX), F32),
            pltpu.VMEM((3, HALF * GROUP, RADIX), F32),
            pltpu.VMEM((2, HALF * GROUP, RADIX), F32),
            pltpu.VMEM((2, 8, 64, 512), F32),
            pltpu.VMEM((8, 64, 512), F32),
            square, square, square,
            dma((2,)), dma((2,)), dma((2,)), dma((4,)), dma((3,)), dma((8, 2, 2)), dma((32,)), dma((8, GROUPS)), dma((28,)),
            dma((2,)), dma((2,)), dma((2,)), dma((4,)), dma((4,)), dma((2,)),
        ],
        compiler_params=pltpu.CompilerParams(
            collective_id=0, has_side_effects=True, vmem_limit_bytes=60 << 20
        ),
        name="gradients",
    )(sent, f, tokens, *tabs)


def body(tokens, queries, keys, values, upstream, filters):
    conv_grad = (upstream[0].astype(F32) * queries[0].astype(F32)).astype(BF16)
    sent = jnp.stack([item.T.reshape(64, 2, 32, RADIX) for item in (conv_grad, keys[0], values[0])], axis=2)
    f = filters.T.reshape(64, HALF, RADIX)
    update, filter_half = gradients(sent, f, tokens[0])
    filter_grad = filter_half.reshape(64, HALF // 2 * RADIX).T
    return (update[None], filter_grad)


def solution(mesh):
    return jax.shard_map(
        body,
        mesh=mesh,
        in_specs=(
            P("dp", "seq", None),
            P("dp", "seq", None),
            P("dp", "seq", None),
            P("dp", "seq", None),
            P("dp", "seq", None),
            P(None, "seq"),
        ),
        out_specs=(P("seq", None, "dp"), P("dp", "seq")),
        check_vma=False,
    )
```

```python
import math

import jax
import jax.numpy as jnp
import numpy as np
from jax import lax
from jax.experimental import pallas as pl
from jax.experimental.pallas import tpu as pltpu
from jax.sharding import PartitionSpec as P

F32, BF16 = jnp.float32, jnp.bfloat16
RADIX = 128
HALF = 64
NS_STEPS = 5
COEF_A = 3.4445
COEF_B = -4.775
COEF_C = 2.0315
ROWS = 72


def split_table(table):
    high = np.asarray(table, np.float32).astype(jnp.bfloat16)
    low = (np.asarray(table, np.float64) - high.astype(np.float64)).astype(jnp.bfloat16)
    return high, low


def fourier_tables():
    total = RADIX * RADIX
    spot = np.arange(RADIX)
    used = np.arange(HALF + 1)
    outer = 2.0 * math.pi * (np.outer(used, np.arange(HALF)) % RADIX) / RADIX
    first = np.zeros((2 * ROWS, HALF))
    first[: HALF + 1] = np.cos(outer)
    first[ROWS : ROWS + HALF + 1] = -np.sin(outer)
    weight = np.where((used == 0) | (used == HALF), 1.0, 2.0)[:, None] / total
    last = np.zeros((2 * ROWS, HALF))
    last[: HALF + 1] = np.cos(outer) * weight
    last[ROWS : ROWS + HALF + 1] = -np.sin(outer) * weight
    last = last.T
    inner = 2.0 * math.pi * (np.outer(spot, spot) % RADIX) / RADIX
    real, imag = np.cos(inner), -np.sin(inner)
    forward = np.block([[real, imag], [-imag, real]])
    turn = 2.0 * math.pi * np.outer(used, spot) / total
    twist = np.zeros((2, ROWS, RADIX), np.float32)
    twist[0, : HALF + 1] = np.cos(turn)
    twist[1, : HALF + 1] = -np.sin(turn)
    first_high, first_low = split_table(first)
    last_high, last_low = split_table(last)
    ahead_high, ahead_low = split_table(forward)
    back_high, back_low = split_table(forward.T)
    return (
        np.concatenate([first_high, first_low, first_high], 1),
        np.concatenate([ahead_high, ahead_high, ahead_low], 0),
        np.concatenate([back_high, back_high, back_low], 0),
        np.concatenate([last_high, last_low, last_high], 1),
        twist,
    )


def dot(left, right):
    return jnp.dot(left, right, preferred_element_type=F32)


def parts(value):
    high = value.astype(BF16)
    return high, (value - high.astype(F32)).astype(BF16)


def convolve_pair(grads, inputs, filters, tables):
    first_ref, ahead_ref, back_ref, last_ref, twist_ref = tables
    turn_real, turn_imag = twist_ref[0], twist_ref[1]
    signals = jnp.concatenate([grads[0], inputs[0], grads[1], inputs[1]], axis=1)
    signals = jnp.concatenate([signals, signals], axis=0)
    spread = dot(first_ref[:, : 2 * HALF], signals)
    high, low = parts(jnp.concatenate(filters, axis=1))
    spread_filter = dot(first_ref[...], jnp.concatenate([high, high, low], axis=0))
    turned = []
    for block in (spread, spread_filter):
        for at in range(0, block.shape[1], RADIX):
            real, imag = block[:ROWS, at : at + RADIX], block[ROWS:, at : at + RADIX]
            turned.append(
                jnp.concatenate(
                    [real * turn_real - imag * turn_imag, real * turn_imag + imag * turn_real], axis=1
                )
            )
    high, low = parts(jnp.concatenate(turned, axis=0))
    spectra = dot(jnp.concatenate([high, low, high], axis=1), ahead_ref[...])
    spec = [
        (spectra[i * ROWS : (i + 1) * ROWS, :RADIX], spectra[i * ROWS : (i + 1) * ROWS, RADIX:])
        for i in range(6)
    ]
    products = []
    for which in range(2):
        grad_real, grad_imag = spec[2 * which]
        input_real, input_imag = spec[2 * which + 1]
        filter_real, filter_imag = spec[4 + which]
        for other_real, other_imag, flip in (
            (filter_real, filter_imag, 0),
            (input_real, input_imag, 0),
        ):
            products.append(
                jnp.concatenate(
                    [
                        grad_real * other_real + grad_imag * other_imag,
                        grad_imag * other_real - grad_real * other_imag,
                    ],
                    axis=1,
                )
            )
    high, low = parts(jnp.concatenate(products, axis=0))
    mixed = dot(jnp.concatenate([high, low, high], axis=1), back_ref[...])
    columns = []
    for i in range(4):
        real, imag = mixed[i * ROWS : (i + 1) * ROWS, :RADIX], mixed[i * ROWS : (i + 1) * ROWS, RADIX:]
        columns.append(
            jnp.concatenate(
                [real * turn_real + imag * turn_imag, imag * turn_real - real * turn_imag], axis=0
            )
        )
    high, low = parts(jnp.concatenate(columns, axis=1))
    result = dot(last_ref[...], jnp.concatenate([high, high, low], axis=0))
    return [result[:, i * RADIX : (i + 1) * RADIX] for i in range(4)]


GROUP = 16


GROUPS = 4


def conv_group(at, stage, in_rows, f_ref, fg_ref, out_rows, tables):
    def pair(j, carry):
        chans = [at + 2 * j, at + 2 * j + 1]
        spots = [pl.ds(2 * j + i, HALF, stride=GROUP) for i in range(2)]
        keys = [in_rows[1, spot, :] for spot in spots]
        values = [in_rows[2, spot, :] for spot in spots]
        inputs = [(a * b).astype(BF16) for a, b in zip(keys, values)]
        grads = [in_rows[0, spot, :].astype(BF16) for spot in spots]
        out = convolve_pair(grads, inputs, [f_ref[chan] for chan in chans], tables)
        for i in range(2):
            back = out[2 * i].astype(BF16).astype(F32)
            fg_ref[chans[i]] = out[2 * i + 1]
            out_rows[0, spots[i], :] = back * values[i]
            out_rows[1, spots[i], :] = back * keys[i]
        return carry

    lax.fori_loop(stage * GROUP // 4, (stage + 1) * GROUP // 4, pair, 0)


STRIDE = 37


def place():
    me = lax.axis_index("seq")
    return me // 32, me // 8 % 4, me // 2 % 4, me % 2


def seq_of(z, x, y, c):
    return ((z * 4 + x) * 4 + y) * 2 + c


def row_block(y, j):
    return y // 2, (y // 2 + j) % 2 * 2 + (y + y // 2) % 2


MESH = pl.DeviceIdType.MESH


def remote(src, dst, send, recv, **device):
    return pltpu.make_async_remote_copy(
        src_ref=src, dst_ref=dst, send_sem=send, recv_sem=recv, device_id=device, device_id_type=MESH
    )


def wait_bytes(ref, sem):
    pltpu.make_async_copy(ref, ref, sem).wait()


def product(left, right):
    left_high, left_low = parts(left)
    right_high, right_low = parts(right)
    left_side = jnp.concatenate([left_high, left_low, left_high], axis=1)
    right_side = jnp.concatenate([right_high, right_high, right_low], axis=0)
    return dot(left_side, right_side)


def gradient_kernel(
    sent, f_ref, tok_ref, t0, t1, t2, t3, t4,
    update_ref, fg_ref,
    got, tok, cols, own, fg_all, fg_in, in_rows, out_rows, part, landed, gram, gram_in, current,
    swap_send, swap_recv, swap_own, tok_first, tok_first_send, tok_recv, tok_send, col_recv, col_send,
    fg_sem, part_send, part_recv, gram_send, gram_recv, final_sem,
):
    tables = (t0, t1, t2, t3, t4)
    z, x, y, c = place()
    me = lax.axis_index("seq")
    dp = lax.axis_index("dp")
    n_seq = lax.axis_size("seq")
    up, down, across = (y + 1) % 4, (y + 3) % 4, (y + 2) % 4
    right, left, far = (x + 1) % 4, (x + 3) % 4, (x + 2) % 4
    sibling = seq_of(z, x, y, 1 - c)
    x_right, x_left = seq_of(z, right, y, c), seq_of(z, left, y, c)
    z_other = seq_of(1 - z, x, y, c)
    mine = (x + y + x // 2) % 2
    kind = (dp + x + y + y // 2) % 2
    side_here = (c + dp) % 2
    finish_x = [x // 2 * 2 + (j + y + x // 2) % 2 for j in range(2)]
    finish_dp = [(c + finish_x[j] + y + y // 2) % 2 for j in range(2)]
    finish_seq = [seq_of(z, finish_x[j], y, (x + finish_dp[j]) % 2) for j in range(2)]
    source_seq = seq_of(z, x // 2 * 2 + side_here, y, kind)
    owner_z, owner_x = row_block(y, mine)
    owner = seq_of(owner_z, owner_x, 2 * kind + z, x // 2)
    owner_dp = side_here
    maker_y = 2 * z + (x + z) % 2
    maker_x = 2 * c + (x // 2 + z + maker_y + c) % 2
    maker_dp = (y // 2 + maker_x + maker_y + z) % 2
    maker = seq_of(y % 2, maker_x, maker_y, (dp + maker_dp) % 2)

    barrier = pltpu.get_barrier_semaphore()

    def greet(d, carry):
        pl.semaphore_signal(barrier, inc=1, device_id={"seq": (me + d) % n_seq}, device_id_type=MESH)
        return carry

    lax.fori_loop(1, n_seq, greet, 0)
    pl.semaphore_signal(barrier, inc=1, device_id={"dp": 1 - dp}, device_id_type=MESH)

    pl.semaphore_signal(barrier, inc=1, device_id={"seq": source_seq, "dp": 1 - dp}, device_id_type=MESH)

    @pl.when(maker_dp != dp)
    def _():
        pl.semaphore_signal(barrier, inc=1, device_id={"seq": maker, "dp": 1 - dp}, device_id_type=MESH)

    pl.semaphore_wait(barrier, n_seq + 1 + (owner_dp + dp) % 2)

    def swap(part_at):
        def one(d, carry):
            peer = (me + STRIDE * d) % n_seq
            remote(
                sent.at[peer, part_at], got.at[part_at, me], swap_send.at[part_at], swap_recv.at[part_at], seq=peer
            ).start()
            return carry

        lax.fori_loop(1, n_seq, one, 0)
        pltpu.make_async_copy(sent.at[me, part_at], got.at[part_at, me], swap_own.at[part_at]).start()

    def wait_swap(part_at):
        wait_bytes(got.at[part_at, pl.ds(0, 63)], swap_recv.at[part_at])
        wait_bytes(got.at[part_at, 0], swap_own.at[part_at])

    swap(0)

    pending = []

    def launch(copy):
        copy.start()
        pending.append(copy)

    here = z * 4 + x

    def quarter(at, j):
        block_z, block_x = row_block(at, j)
        return tok_ref.at[:, pl.ds(pl.multiple_of((block_z * 4 + block_x) * 512, 512), 512)]

    def spot(j):
        return tok.at[here, c, y, :, pl.ds(512 * j, 512)]

    for j in range(2):
        for i, target in enumerate((up, down, across)):
            launch(
                remote(
                    quarter(target, j), spot(j), tok_first_send.at[2 * i + j], tok_first.at[i, j],
                    seq=seq_of(z, x, target, c),
                )
            )
        pltpu.make_async_copy(quarter(y, j), spot(j), tok_first.at[3, j]).start()
    swap(1)

    count = [0]

    def half(zz, xx, cc, h):
        return tok.at[zz * 4 + xx, cc, pl.ds(2 * h, 2)]

    def send_half(zz, xx, h, target):
        launch(
            remote(
                half(zz, xx, c, h), half(zz, xx, c, h), tok_send.at[count[0]],
                tok_recv.at[zz * 4 + xx, c, h], seq=target,
            )
        )
        count[0] += 1

    def wait_half(zz, xx, cc, h):
        wait_bytes(half(zz, xx, cc, h), tok_recv.at[zz * 4 + xx, cc, h])

    def wait_first():
        for i, source_y in ((0, down), (1, up), (2, across), (3, y)):
            for j in range(2):
                wait_bytes(tok.at[here, c, source_y, :, pl.ds(512 * j, 512)], tok_first.at[i, j])

    def spread(zz):
        for a, b in ((0, 1), (1, 0)):
            send_half(zz, x, a, x_right)
            send_half(zz, x, b, x_left)

    def relay(zz):
        wait_half(zz, left, c, 0)
        send_half(zz, left, 0, x_right)
        wait_half(zz, right, c, 1)
        send_half(zz, right, 1, x_left)

    def share(zz, xx, h):
        send_half(zz, xx, h, sibling)

    def slot(yy, cc, i):
        return (yy * 2 + cc, i)

    def send_group(i):
        mine = cols.at[slot(y, c, i)]
        arrival = col_recv.at[slot(y, c, i)]
        for n, (kind, target) in enumerate(((0, up), (1, up), (0, down), (1, down))):
            launch(
                remote(own.at[kind, i], mine, col_send.at[i * 5 + n], arrival, seq=seq_of(z, x, target, kind))
            )
        launch(remote(own.at[1 - c, i], mine, col_send.at[i * 5 + 4], arrival, seq=sibling))
        pltpu.make_async_copy(own.at[c, i], mine, arrival).start()

    def wait_col(at):
        wait_bytes(cols.at[at], col_recv.at[at])

    forwarded = [0]

    def relay_group(i):
        source_y, target = (down, up) if i % 2 == 0 else (up, down)
        for cc in range(2):
            at = slot(source_y, cc, i)
            wait_col(at)
            launch(
                remote(
                    cols.at[at], cols.at[at], col_send.at[5 * GROUPS + forwarded[0]], col_recv.at[at],
                    seq=seq_of(z, x, target, c),
                )
            )
            forwarded[0] += 1

    def compute(i, stage):
        if stage == 0:
            for kind in range(3):
                chunk = got[i // 2, :, kind, pl.ds(GROUP * (i % 2), GROUP), :]
                in_rows[kind] = chunk.astype(F32).reshape(HALF * GROUP, RADIX)
        conv_group(i * GROUP, stage, in_rows, f_ref, fg_all, out_rows, tables)
        if stage == 1:
            for kind in range(2):
                own[kind, i] = out_rows[kind].reshape(HALF, GROUP, RADIX).astype(BF16)
            send_group(i)

    wait_swap(0)
    compute(0, 0)
    wait_first()
    spread(z)
    for h in range(2):
        send_half(z, x, h, z_other)
        share(z, x, h)
    compute(0, 1)
    compute(1, 0)
    relay(z)
    compute(1, 1)
    wait_swap(1)
    relay_group(0)
    compute(2, 0)
    for h in range(2):
        wait_half(1 - z, x, c, h)
    spread(1 - z)
    for xx, h in ((left, 0), (right, 1)):
        share(z, xx, h)
    compute(2, 1)
    relay_group(1)
    for xx, h in ((left, 1), (right, 0)):
        wait_half(z, xx, c, h)
        share(z, xx, h)
    for h in range(2):
        share(1 - z, x, h)
    compute(3, 0)
    for h in range(2):
        wait_half(z, far, c, h)
        share(z, far, h)
    relay(1 - z)
    compute(3, 1)
    fg_copy = remote(
        fg_all.at[:, pl.ds((1 - dp) * 32, 32)], fg_in, fg_sem.at[0], fg_sem.at[1], dp=1 - dp
    )
    launch(fg_copy)
    def wait_group(i):
        for cc in range(2):
            wait_col(slot(y, cc, i))
            wait_col(slot(across, cc, i))
            wait_col(slot(up if i % 2 == 0 else down, cc, i))

    def multiply(zx, side, fresh):
        left_side = jnp.concatenate(
            [
                cols[:, pl.ds(2 * side, 2), zx * 8 + yy * 2 + cc].reshape(256, RADIX)
                for cc in range(2)
                for yy in range(4)
            ],
            axis=1,
        )

        def tile(n, carry):
            j, at = n // 2, pl.multiple_of(n % 2 * 256, 256)
            right_side = tok[zx, :, :, :, pl.ds(pl.multiple_of(n * 256, 256), 256)].reshape(1024, 256)
            term = dot(left_side, right_side).reshape(8, 32, 256)
            if fresh:
                part[j, :, pl.ds(32 * side, 32), pl.ds(at, 256)] = term
            else:
                part[j, :, pl.ds(32 * side, 32), pl.ds(at, 256)] += term
            return carry

        lax.fori_loop(0, 4, tile, 0)

    stays = [jnp.logical_and(finish_seq[j] == me, finish_dp[j] == dp) for j in range(2)]

    def part_copy(j, side):
        view = (slice(None), pl.ds(32 * side, 32))
        src, dst, arrival = part.at[(j, *view)], landed.at[(dp, *view)], part_recv.at[dp, side]
        return (
            remote(src, dst, part_send.at[j, side], arrival, seq=finish_seq[j], dp=finish_dp[j]),
            pltpu.make_async_copy(src, dst, arrival),
        )

    def send_parts(side):
        for j in range(2):
            away, at_home = part_copy(j, side)

            @pl.when(stays[j])
            def _():
                at_home.start()

            @pl.when(jnp.logical_not(stays[j]))
            def _():
                away.start()

    def multiply_all(zz, side, fresh):
        if fresh:
            multiply(zz * 4 + x, side, True)

        def more(i, carry):
            multiply(zz * 4 + (x + i) % 4, side, False)
            return carry

        lax.fori_loop(1 if fresh else 0, 4, more, 0)

    def wait_tokens(zz):
        for xx in (x, left, right, far):
            for h in range(2):
                wait_half(zz, xx, 1 - c, h)

    relay_group(2)
    wait_group(0)
    wait_group(1)
    wait_tokens(z)
    for xx, h in ((left, 0), (right, 1)):
        share(1 - z, xx, h)
    for xx, h in ((left, 1), (right, 0)):
        wait_half(1 - z, xx, c, h)
        share(1 - z, xx, h)
    relay_group(3)
    multiply_all(z, 0, True)
    for h in range(2):
        wait_half(1 - z, far, c, h)
        share(1 - z, far, h)
    wait_tokens(1 - z)
    multiply_all(1 - z, 0, False)
    send_parts(0)
    wait_group(2)
    wait_group(3)
    multiply_all(z, 1, True)
    multiply_all(1 - z, 1, False)
    send_parts(1)
    fg_copy.wait_recv()
    fg_ref[...] = fg_all[:, pl.ds(dp * 32, 32)] + fg_in[...]

    for side in range(2):
        for d in range(2):
            wait_bytes(landed.at[d, :, pl.ds(32 * side, 32)], part_recv.at[d, side])
        columns = landed[0, :, pl.ds(32 * side, 32), :] + landed[1, :, pl.ds(32 * side, 32), :]
        columns = columns.reshape(256, 512)
        term = product(columns.T, columns)
        if side == 0:
            gram[...] = term
        else:
            gram[...] += term
    exchanges = []
    for i in range(4):
        view = (pl.ds(128 * i, 128), pl.ds(128 * i, 512 - 128 * i))
        copy = remote(gram.at[view], gram_in.at[view], gram_send.at[i], gram_recv.at[i], seq=sibling)
        launch(copy)
        exchanges.append(copy)
    current[...] = (landed[0] + landed[1]).reshape(512, 512).T
    for copy in exchanges:
        copy.wait_recv()
    diagonal = lax.broadcasted_iota(jnp.int32, (128, 128), 0) == lax.broadcasted_iota(jnp.int32, (128, 128), 1)
    trace = jnp.zeros((1, 1), F32)
    for i in range(4):
        block = gram[128 * i : 128 * (i + 1), 128 * i : 128 * (i + 1)]
        block = block + gram_in[128 * i : 128 * (i + 1), 128 * i : 128 * (i + 1)]
        trace = trace + jnp.sum(jnp.where(diagonal, block, 0.0), keepdims=True)
    scale = 1.0 / (jnp.sqrt(trace) + 1e-07)
    for i in range(4):
        for j in range(i, 4):
            at = (slice(128 * i, 128 * (i + 1)), slice(128 * j, 128 * (j + 1)))
            block = (gram[at] + gram_in[at]) * scale * scale
            gram_in[at] = block
            if j > i:
                gram_in[at[1], at[0]] = block.T
    current[...] = current[...] * scale

    def step(i, carry):
        gram_now = gram_in[...]
        mixer = COEF_B * gram_now + COEF_C * product(gram_now, gram_now)
        current[...] = COEF_A * current[...] + product(mixer, current[...])
        half_step = COEF_A * gram_now + product(mixer, gram_now)
        gram_in[...] = COEF_A * half_step + product(half_step, mixer)
        return carry

    lax.fori_loop(0, NS_STEPS - 1, step, 0)
    gram_now = gram_in[...]
    mixer = COEF_B * gram_now + COEF_C * product(gram_now, gram_now)
    current[...] = (COEF_A * current[...] + product(mixer, current[...])) * 32.0
    is_owner = jnp.logical_and(owner == me, owner_dp == dp)
    away = remote(current, update_ref, final_sem.at[0], final_sem.at[1], seq=owner, dp=owner_dp)

    @pl.when(is_owner)
    def _():
        pltpu.make_async_copy(current, update_ref, final_sem.at[1]).start()

    @pl.when(jnp.logical_not(is_owner))
    def _():
        away.start()

    wait_bytes(update_ref, final_sem.at[1])

    @pl.when(jnp.logical_not(is_owner))
    def _():
        away.wait_send()

    for side in range(2):
        for j in range(2):
            away, _ = part_copy(j, side)

            @pl.when(jnp.logical_not(stays[j]))
            def _():
                away.wait_send()

    for i in range(2):
        wait_bytes(got.at[i, pl.ds(0, 63)], swap_send.at[i])
    for copy in pending:
        copy.wait_send()


def gradients(sent, f, tokens):
    tabs = [jnp.asarray(t) for t in fourier_tables()]
    vm = pl.BlockSpec(memory_space=pltpu.VMEM)
    dma = pltpu.SemaphoreType.DMA
    square = pltpu.VMEM((512, 512), F32)
    return pl.pallas_call(
        gradient_kernel,
        out_shape=(
            jax.ShapeDtypeStruct((512, 512), F32),
            jax.ShapeDtypeStruct((64, HALF // 2, RADIX), F32),
        ),
        in_specs=[vm] * 8,
        out_specs=[vm] * 2,
        scratch_shapes=[
            pltpu.VMEM((2, 64, 3, 32, RADIX), BF16),
            pltpu.VMEM((8, 2, 4, RADIX, 1024), BF16),
            pltpu.VMEM((8, GROUPS, HALF, GROUP, RADIX), BF16),
            pltpu.VMEM((2, GROUPS, HALF, GROUP, RADIX), BF16),
            pltpu.VMEM((64, HALF, RADIX), F32),
            pltpu.VMEM((64, HALF // 2, RADIX), F32),
            pltpu.VMEM((3, HALF * GROUP, RADIX), F32),
            pltpu.VMEM((2, HALF * GROUP, RADIX), F32),
            pltpu.VMEM((2, 8, 64, 512), F32),
            pltpu.VMEM((2, 8, 64, 512), F32),
            square, square, square,
            dma((2,)), dma((2,)), dma((2,)), dma((4, 2)), dma((6,)), dma((8, 2, 2)), dma((32,)), dma((8, GROUPS)), dma((28,)),
            dma((2,)), dma((2, 2)), dma((2, 2)), dma((4,)), dma((4,)), dma((2,)),
        ],
        compiler_params=pltpu.CompilerParams(
            collective_id=0, has_side_effects=True, vmem_limit_bytes=60 << 20
        ),
        name="gradients",
    )(sent, f, tokens, *tabs)


def body(tokens, queries, keys, values, upstream, filters):
    conv_grad = (upstream[0].astype(F32) * queries[0].astype(F32)).astype(BF16)
    sent = jnp.stack([item.T.reshape(64, 2, 32, RADIX) for item in (conv_grad, keys[0], values[0])], axis=2)
    f = filters.T.reshape(64, HALF, RADIX)
    update, filter_half = gradients(sent, f, tokens[0])
    filter_grad = filter_half.reshape(64, HALF // 2 * RADIX).T
    return (update[None], filter_grad)


def solution(mesh):
    return jax.shard_map(
        body,
        mesh=mesh,
        in_specs=(
            P("dp", "seq", None),
            P("dp", "seq", None),
            P("dp", "seq", None),
            P("dp", "seq", None),
            P("dp", "seq", None),
            P(None, "seq"),
        ),
        out_specs=(P("seq", None, "dp"), P("dp", "seq")),
        check_vma=False,
    )
```

```python
import math

import jax
import jax.numpy as jnp
import numpy as np
from jax import lax
from jax.experimental import pallas as pl
from jax.experimental.pallas import tpu as pltpu
from jax.sharding import PartitionSpec as P

F32, BF16 = jnp.float32, jnp.bfloat16
RADIX = 128
HALF = 64
NS_STEPS = 5
COEF_A = 3.4445
COEF_B = -4.775
COEF_C = 2.0315
ROWS = 72


def split_table(table):
    high = np.asarray(table, np.float32).astype(jnp.bfloat16)
    low = (np.asarray(table, np.float64) - high.astype(np.float64)).astype(jnp.bfloat16)
    return high, low


def fourier_tables():
    total = RADIX * RADIX
    spot = np.arange(RADIX)
    used = np.arange(HALF + 1)
    outer = 2.0 * math.pi * (np.outer(used, np.arange(HALF)) % RADIX) / RADIX
    first = np.zeros((2 * ROWS, HALF))
    first[: HALF + 1] = np.cos(outer)
    first[ROWS : ROWS + HALF + 1] = -np.sin(outer)
    weight = np.where((used == 0) | (used == HALF), 1.0, 2.0)[:, None] / total
    last = np.zeros((2 * ROWS, HALF))
    last[: HALF + 1] = np.cos(outer) * weight
    last[ROWS : ROWS + HALF + 1] = -np.sin(outer) * weight
    last = last.T
    inner = 2.0 * math.pi * (np.outer(spot, spot) % RADIX) / RADIX
    real, imag = np.cos(inner), -np.sin(inner)
    forward = np.block([[real, imag], [-imag, real]])
    turn = 2.0 * math.pi * np.outer(used, spot) / total
    twist = np.zeros((2, ROWS, RADIX), np.float32)
    twist[0, : HALF + 1] = np.cos(turn)
    twist[1, : HALF + 1] = -np.sin(turn)
    first_high, first_low = split_table(first)
    last_high, last_low = split_table(last)
    ahead_high, ahead_low = split_table(forward)
    back_high, back_low = split_table(forward.T)
    return (
        np.concatenate([first_high, first_low, first_high], 1),
        np.concatenate([ahead_high, ahead_high, ahead_low], 0),
        np.concatenate([back_high, back_high, back_low], 0),
        np.concatenate([last_high, last_low, last_high], 1),
        twist,
    )


def dot(left, right):
    return jnp.dot(left, right, preferred_element_type=F32)


def parts(value):
    high = value.astype(BF16)
    return high, (value - high.astype(F32)).astype(BF16)


def convolve_pair(grads, inputs, filters, tables):
    first_ref, ahead_ref, back_ref, last_ref, twist_ref = tables
    turn_real, turn_imag = twist_ref[0], twist_ref[1]
    signals = jnp.concatenate([grads[0], inputs[0], grads[1], inputs[1]], axis=1)
    signals = jnp.concatenate([signals, signals], axis=0)
    spread = dot(first_ref[:, : 2 * HALF], signals)
    high, low = parts(jnp.concatenate(filters, axis=1))
    spread_filter = dot(first_ref[...], jnp.concatenate([high, high, low], axis=0))
    turned = []
    for block in (spread, spread_filter):
        for at in range(0, block.shape[1], RADIX):
            real, imag = block[:ROWS, at : at + RADIX], block[ROWS:, at : at + RADIX]
            turned.append(
                jnp.concatenate(
                    [real * turn_real - imag * turn_imag, real * turn_imag + imag * turn_real], axis=1
                )
            )
    high, low = parts(jnp.concatenate(turned, axis=0))
    spectra = dot(jnp.concatenate([high, low, high], axis=1), ahead_ref[...])
    spec = [
        (spectra[i * ROWS : (i + 1) * ROWS, :RADIX], spectra[i * ROWS : (i + 1) * ROWS, RADIX:])
        for i in range(6)
    ]
    products = []
    for which in range(2):
        grad_real, grad_imag = spec[2 * which]
        input_real, input_imag = spec[2 * which + 1]
        filter_real, filter_imag = spec[4 + which]
        for other_real, other_imag, flip in (
            (filter_real, filter_imag, 0),
            (input_real, input_imag, 0),
        ):
            products.append(
                jnp.concatenate(
                    [
                        grad_real * other_real + grad_imag * other_imag,
                        grad_imag * other_real - grad_real * other_imag,
                    ],
                    axis=1,
                )
            )
    high, low = parts(jnp.concatenate(products, axis=0))
    mixed = dot(jnp.concatenate([high, low, high], axis=1), back_ref[...])
    columns = []
    for i in range(4):
        real, imag = mixed[i * ROWS : (i + 1) * ROWS, :RADIX], mixed[i * ROWS : (i + 1) * ROWS, RADIX:]
        columns.append(
            jnp.concatenate(
                [real * turn_real + imag * turn_imag, imag * turn_real - real * turn_imag], axis=0
            )
        )
    high, low = parts(jnp.concatenate(columns, axis=1))
    result = dot(last_ref[...], jnp.concatenate([high, high, low], axis=0))
    return [result[:, i * RADIX : (i + 1) * RADIX] for i in range(4)]


GROUP = 16


GROUPS = 4


def conv_group(at, stage, in_rows, fg_rows, out_rows, tables):
    def pair(j, carry):
        chans = [at + 2 * j, at + 2 * j + 1]
        spots = [pl.ds(2 * j + i, HALF, stride=GROUP) for i in range(2)]
        keys = [in_rows[1, spot, :] for spot in spots]
        values = [in_rows[2, spot, :] for spot in spots]
        inputs = [(a * b).astype(BF16) for a, b in zip(keys, values)]
        grads = [in_rows[0, spot, :].astype(BF16) for spot in spots]
        out = convolve_pair(grads, inputs, [in_rows[3, spot, :] for spot in spots], tables)
        for i in range(2):
            back = out[2 * i].astype(BF16).astype(F32)
            fg_rows[pl.ds(chans[i], HALF, stride=64), :] = out[2 * i + 1]
            out_rows[0, spots[i], :] = back * values[i]
            out_rows[1, spots[i], :] = back * keys[i]
        return carry

    lax.fori_loop(stage * GROUP // 4, (stage + 1) * GROUP // 4, pair, 0)


STRIDE = 37


def place():
    me = lax.axis_index("seq")
    return me // 32, me // 8 % 4, me // 2 % 4, me % 2


def seq_of(z, x, y, c):
    return ((z * 4 + x) * 4 + y) * 2 + c


def row_block(y, j):
    return y // 2, (y // 2 + j) % 2 * 2 + (y + y // 2) % 2


MESH = pl.DeviceIdType.MESH


def remote(src, dst, send, recv, **device):
    return pltpu.make_async_remote_copy(
        src_ref=src, dst_ref=dst, send_sem=send, recv_sem=recv, device_id=device, device_id_type=MESH
    )


def wait_bytes(ref, sem):
    pltpu.make_async_copy(ref, ref, sem).wait()


def product(left, right):
    left_high, left_low = parts(left)
    right_high, right_low = parts(right)
    left_side = jnp.concatenate([left_high, left_low, left_high], axis=1)
    right_side = jnp.concatenate([right_high, right_high, right_low], axis=0)
    return dot(left_side, right_side)


def gradient_kernel(
    up_ref, q_ref, k_ref, v_ref, f_ref, tok_ref, t0, t1, t2, t3, t4,
    update_ref, fg_ref,
    sent, got, tok, cols, own, fg_all, fg_in, in_rows, out_rows, part, landed, gram, gram_in, current,
    swap_send, swap_recv, swap_own, tok_first, tok_first_send, tok_recv, tok_send, col_recv, col_send,
    fg_sem, part_send, part_recv, gram_send, gram_recv, final_sem,
):
    tables = (t0, t1, t2, t3, t4)
    z, x, y, c = place()
    me = lax.axis_index("seq")
    dp = lax.axis_index("dp")
    n_seq = lax.axis_size("seq")
    up, down, across = (y + 1) % 4, (y + 3) % 4, (y + 2) % 4
    right, left, far = (x + 1) % 4, (x + 3) % 4, (x + 2) % 4
    sibling = seq_of(z, x, y, 1 - c)
    x_right, x_left = seq_of(z, right, y, c), seq_of(z, left, y, c)
    z_other = seq_of(1 - z, x, y, c)
    mine = (x + y + x // 2) % 2
    kind = (dp + x + y + y // 2) % 2
    side_here = (c + dp) % 2
    finish_x = [x // 2 * 2 + (j + y + x // 2) % 2 for j in range(2)]
    finish_dp = [(c + finish_x[j] + y + y // 2) % 2 for j in range(2)]
    finish_seq = [seq_of(z, finish_x[j], y, (x + finish_dp[j]) % 2) for j in range(2)]
    source_seq = seq_of(z, x // 2 * 2 + side_here, y, kind)
    owner_z, owner_x = row_block(y, mine)
    owner = seq_of(owner_z, owner_x, 2 * kind + z, x // 2)
    owner_dp = side_here
    maker_y = 2 * z + (x + z) % 2
    maker_x = 2 * c + (x // 2 + z + maker_y + c) % 2
    maker_dp = (y // 2 + maker_x + maker_y + z) % 2
    maker = seq_of(y % 2, maker_x, maker_y, (dp + maker_dp) % 2)

    barrier = pltpu.get_barrier_semaphore()

    def greet(d, carry):
        pl.semaphore_signal(barrier, inc=1, device_id={"seq": (me + d) % n_seq}, device_id_type=MESH)
        return carry

    lax.fori_loop(1, n_seq, greet, 0)
    pl.semaphore_signal(barrier, inc=1, device_id={"dp": 1 - dp}, device_id_type=MESH)

    pl.semaphore_signal(barrier, inc=1, device_id={"seq": source_seq, "dp": 1 - dp}, device_id_type=MESH)

    @pl.when(maker_dp != dp)
    def _():
        pl.semaphore_signal(barrier, inc=1, device_id={"seq": maker, "dp": 1 - dp}, device_id_type=MESH)

    pl.semaphore_wait(barrier, n_seq + 1 + (owner_dp + dp) % 2)

    def swap_piece(peer, part_at):
        return remote(
            sent.at[peer, part_at], got.at[part_at, me], swap_send.at[part_at], swap_recv.at[part_at], seq=peer
        )

    def swap_here(part_at):
        return pltpu.make_async_copy(sent.at[me, part_at], got.at[part_at, me], swap_own.at[part_at])

    def prepare(chip):
        span = pl.ds(pl.multiple_of(chip * RADIX, RADIX), RADIX)
        conv_grad = up_ref[:, span].astype(F32) * q_ref[:, span].astype(F32)
        for kind, item in enumerate((conv_grad, k_ref[:, span].astype(F32), v_ref[:, span].astype(F32))):
            turned = item.T.astype(BF16)
            for core in range(2):
                for part_at in range(2):
                    at = 64 * core + 32 * part_at
                    sent[2 * chip + core, part_at, kind] = turned[at : at + 32]

    def first_half(i, carry):
        chip = (me // 2 + 19 * i) % (n_seq // 2)
        prepare(chip)
        for core in range(2):
            swap_piece(2 * chip + core, 0).start()
        return carry

    def second_half(d, carry):
        swap_piece((me + STRIDE * d) % n_seq, 1).start()
        return carry

    def wait_swap(part_at):
        wait_bytes(got.at[part_at, pl.ds(0, 63)], swap_recv.at[part_at])
        wait_bytes(got.at[part_at, 0], swap_own.at[part_at])

    prepare(me // 2)
    swap_piece(sibling, 0).start()
    for part_at in range(2):
        swap_here(part_at).start()
    lax.fori_loop(1, n_seq // 2, first_half, 0)

    pending = []

    def launch(copy):
        copy.start()
        pending.append(copy)

    here = z * 4 + x

    def quarter(at, j):
        block_z, block_x = row_block(at, j)
        return tok_ref.at[:, pl.ds(pl.multiple_of((block_z * 4 + block_x) * 512, 512), 512)]

    def spot(j):
        return tok.at[here, c, y, :, pl.ds(512 * j, 512)]

    for j in range(2):
        for i, target in enumerate((up, down, across)):
            launch(
                remote(
                    quarter(target, j), spot(j), tok_first_send.at[2 * i + j], tok_first.at[i, j],
                    seq=seq_of(z, x, target, c),
                )
            )
        pltpu.make_async_copy(quarter(y, j), spot(j), tok_first.at[3, j]).start()
    lax.fori_loop(1, n_seq, second_half, 0)

    count = [0]

    def half(zz, xx, cc, h):
        return tok.at[zz * 4 + xx, cc, pl.ds(2 * h, 2)]

    def send_half(zz, xx, h, target):
        launch(
            remote(
                half(zz, xx, c, h), half(zz, xx, c, h), tok_send.at[count[0]],
                tok_recv.at[zz * 4 + xx, c, h], seq=target,
            )
        )
        count[0] += 1

    def wait_half(zz, xx, cc, h):
        wait_bytes(half(zz, xx, cc, h), tok_recv.at[zz * 4 + xx, cc, h])

    def wait_first():
        for i, source_y in ((0, down), (1, up), (2, across), (3, y)):
            for j in range(2):
                wait_bytes(tok.at[here, c, source_y, :, pl.ds(512 * j, 512)], tok_first.at[i, j])

    def spread(zz):
        for a, b in ((0, 1), (1, 0)):
            send_half(zz, x, a, x_right)
            send_half(zz, x, b, x_left)

    def relay(zz):
        wait_half(zz, left, c, 0)
        send_half(zz, left, 0, x_right)
        wait_half(zz, right, c, 1)
        send_half(zz, right, 1, x_left)

    def share(zz, xx, h):
        send_half(zz, xx, h, sibling)

    def slot(yy, cc, i):
        return (yy * 2 + cc, i)

    def send_group(i):
        mine = cols.at[slot(y, c, i)]
        arrival = col_recv.at[slot(y, c, i)]
        for n, (kind, target) in enumerate(((0, up), (1, up), (0, down), (1, down))):
            launch(
                remote(own.at[kind, i], mine, col_send.at[i * 5 + n], arrival, seq=seq_of(z, x, target, kind))
            )
        launch(remote(own.at[1 - c, i], mine, col_send.at[i * 5 + 4], arrival, seq=sibling))
        pltpu.make_async_copy(own.at[c, i], mine, arrival).start()

    def wait_col(at):
        wait_bytes(cols.at[at], col_recv.at[at])

    forwarded = [0]

    def relay_group(i):
        source_y, target = (down, up) if i % 2 == 0 else (up, down)
        for cc in range(2):
            at = slot(source_y, cc, i)
            wait_col(at)
            launch(
                remote(
                    cols.at[at], cols.at[at], col_send.at[5 * GROUPS + forwarded[0]], col_recv.at[at],
                    seq=seq_of(z, x, target, c),
                )
            )
            forwarded[0] += 1

    def compute(i, stage):
        if stage == 0:
            for kind in range(3):
                chunk = got[i // 2, :, kind, pl.ds(GROUP * (i % 2), GROUP), :]
                in_rows[kind] = chunk.astype(F32).reshape(HALF * GROUP, RADIX)
            for n in range(HALF):
                in_rows[3, GROUP * n : GROUP * (n + 1), :] = f_ref[
                    GROUP * i : GROUP * (i + 1), RADIX * n : RADIX * (n + 1)
                ]
        conv_group(i * GROUP, stage, in_rows, fg_all, out_rows, tables)
        if stage == 1:
            for kind in range(2):
                own[kind, i] = out_rows[kind].reshape(HALF, GROUP, RADIX).astype(BF16)
            send_group(i)

    wait_swap(0)
    compute(0, 0)
    wait_first()
    spread(z)
    for h in range(2):
        send_half(z, x, h, z_other)
        share(z, x, h)
    compute(0, 1)
    compute(1, 0)
    relay(z)
    compute(1, 1)
    wait_swap(1)
    relay_group(0)
    compute(2, 0)
    for h in range(2):
        wait_half(1 - z, x, c, h)
    spread(1 - z)
    for xx, h in ((left, 0), (right, 1)):
        share(z, xx, h)
    compute(2, 1)
    relay_group(1)
    for xx, h in ((left, 1), (right, 0)):
        wait_half(z, xx, c, h)
        share(z, xx, h)
    for h in range(2):
        share(1 - z, x, h)
    compute(3, 0)
    for h in range(2):
        wait_half(z, far, c, h)
        share(z, far, h)
    relay(1 - z)
    compute(3, 1)
    fg_copy = remote(
        fg_all.at[pl.ds(pl.multiple_of((1 - dp) * 2048, 2048), 2048)], fg_in, fg_sem.at[0], fg_sem.at[1], dp=1 - dp
    )
    launch(fg_copy)
    def wait_group(i):
        for cc in range(2):
            wait_col(slot(y, cc, i))
            wait_col(slot(across, cc, i))
            wait_col(slot(up if i % 2 == 0 else down, cc, i))

    def multiply(zx, side, fresh):
        left_side = jnp.concatenate(
            [
                cols[:, pl.ds(2 * side, 2), zx * 8 + yy * 2 + cc].reshape(256, RADIX)
                for cc in range(2)
                for yy in range(4)
            ],
            axis=1,
        )

        def tile(n, carry):
            j, at = n // 2, pl.multiple_of(n % 2 * 256, 256)
            right_side = tok[zx, :, :, :, pl.ds(pl.multiple_of(n * 256, 256), 256)].reshape(1024, 256)
            term = dot(left_side, right_side).reshape(8, 32, 256)
            if fresh:
                part[j, :, pl.ds(32 * side, 32), pl.ds(at, 256)] = term
            else:
                part[j, :, pl.ds(32 * side, 32), pl.ds(at, 256)] += term
            return carry

        lax.fori_loop(0, 4, tile, 0)

    stays = [jnp.logical_and(finish_seq[j] == me, finish_dp[j] == dp) for j in range(2)]

    def part_copy(j, side):
        view = (slice(None), pl.ds(32 * side, 32))
        src, dst, arrival = part.at[(j, *view)], landed.at[(dp, *view)], part_recv.at[dp, side]
        return (
            remote(src, dst, part_send.at[j, side], arrival, seq=finish_seq[j], dp=finish_dp[j]),
            pltpu.make_async_copy(src, dst, arrival),
        )

    def send_parts(side):
        for j in range(2):
            away, at_home = part_copy(j, side)

            @pl.when(stays[j])
            def _():
                at_home.start()

            @pl.when(jnp.logical_not(stays[j]))
            def _():
                away.start()

    def multiply_all(zz, side, fresh):
        if fresh:
            multiply(zz * 4 + x, side, True)

        def more(i, carry):
            multiply(zz * 4 + (x + i) % 4, side, False)
            return carry

        lax.fori_loop(1 if fresh else 0, 4, more, 0)

    def wait_tokens(zz):
        for xx in (x, left, right, far):
            for h in range(2):
                wait_half(zz, xx, 1 - c, h)

    relay_group(2)
    wait_group(0)
    wait_group(1)
    wait_tokens(z)
    for xx, h in ((left, 0), (right, 1)):
        share(1 - z, xx, h)
    for xx, h in ((left, 1), (right, 0)):
        wait_half(1 - z, xx, c, h)
        share(1 - z, xx, h)
    relay_group(3)
    multiply_all(z, 0, True)
    for h in range(2):
        wait_half(1 - z, far, c, h)
        share(1 - z, far, h)
    wait_tokens(1 - z)
    multiply_all(1 - z, 0, False)
    send_parts(0)
    wait_group(2)
    wait_group(3)
    multiply_all(z, 1, True)
    multiply_all(1 - z, 1, False)
    send_parts(1)
    fg_copy.wait_recv()
    for n in range(HALF // 2):
        kept = fg_all[pl.ds(pl.multiple_of(dp * 2048 + 64 * n, 64), 64), :]
        fg_ref[:, RADIX * n : RADIX * (n + 1)] = kept + fg_in[64 * n : 64 * (n + 1), :]

    for side in range(2):
        for d in range(2):
            wait_bytes(landed.at[d, :, pl.ds(32 * side, 32)], part_recv.at[d, side])
        columns = landed[0, :, pl.ds(32 * side, 32), :] + landed[1, :, pl.ds(32 * side, 32), :]
        columns = columns.reshape(256, 512)
        term = product(columns.T, columns)
        if side == 0:
            gram[...] = term
        else:
            gram[...] += term
    exchanges = []
    for i in range(4):
        view = (pl.ds(128 * i, 128), pl.ds(128 * i, 512 - 128 * i))
        copy = remote(gram.at[view], gram_in.at[view], gram_send.at[i], gram_recv.at[i], seq=sibling)
        launch(copy)
        exchanges.append(copy)
    current[...] = (landed[0] + landed[1]).reshape(512, 512).T
    for copy in exchanges:
        copy.wait_recv()
    diagonal = lax.broadcasted_iota(jnp.int32, (128, 128), 0) == lax.broadcasted_iota(jnp.int32, (128, 128), 1)
    trace = jnp.zeros((1, 1), F32)
    for i in range(4):
        block = gram[128 * i : 128 * (i + 1), 128 * i : 128 * (i + 1)]
        block = block + gram_in[128 * i : 128 * (i + 1), 128 * i : 128 * (i + 1)]
        trace = trace + jnp.sum(jnp.where(diagonal, block, 0.0), keepdims=True)
    scale = 1.0 / (jnp.sqrt(trace) + 1e-07)
    for i in range(4):
        for j in range(i, 4):
            at = (slice(128 * i, 128 * (i + 1)), slice(128 * j, 128 * (j + 1)))
            block = (gram[at] + gram_in[at]) * scale * scale
            gram_in[at] = block
            if j > i:
                gram_in[at[1], at[0]] = block.T
    current[...] = current[...] * scale

    def step(i, carry):
        gram_now = gram_in[...]
        mixer = COEF_B * gram_now + COEF_C * product(gram_now, gram_now)
        current[...] = COEF_A * current[...] + product(mixer, current[...])
        half_step = COEF_A * gram_now + product(mixer, gram_now)
        gram_in[...] = COEF_A * half_step + product(half_step, mixer)
        return carry

    lax.fori_loop(0, NS_STEPS - 1, step, 0)
    gram_now = gram_in[...]
    mixer = COEF_B * gram_now + COEF_C * product(gram_now, gram_now)
    current[...] = COEF_A * current[...] + product(mixer, current[...])
    is_owner = jnp.logical_and(owner == me, owner_dp == dp)
    away = remote(current, update_ref, final_sem.at[0], final_sem.at[1], seq=owner, dp=owner_dp)

    @pl.when(is_owner)
    def _():
        pltpu.make_async_copy(current, update_ref, final_sem.at[1]).start()

    @pl.when(jnp.logical_not(is_owner))
    def _():
        away.start()

    wait_bytes(update_ref, final_sem.at[1])

    @pl.when(jnp.logical_not(is_owner))
    def _():
        away.wait_send()

    for side in range(2):
        for j in range(2):
            away, _ = part_copy(j, side)

            @pl.when(jnp.logical_not(stays[j]))
            def _():
                away.wait_send()

    for i in range(2):
        wait_bytes(got.at[i, pl.ds(0, 63)], swap_send.at[i])
    for copy in pending:
        copy.wait_send()


def gradients(upstream, queries, keys, values, f, tokens):
    tabs = [jnp.asarray(t) for t in fourier_tables()]
    vm = pl.BlockSpec(memory_space=pltpu.VMEM)
    dma = pltpu.SemaphoreType.DMA
    square = pltpu.VMEM((512, 512), F32)
    return pl.pallas_call(
        gradient_kernel,
        out_shape=(
            jax.ShapeDtypeStruct((512, 512), F32),
            jax.ShapeDtypeStruct((64, HALF // 2 * RADIX), F32),
        ),
        in_specs=[vm] * 11,
        out_specs=[vm] * 2,
        scratch_shapes=[
            pltpu.VMEM((64, 2, 3, 32, RADIX), BF16),
            pltpu.VMEM((2, 64, 3, 32, RADIX), BF16),
            pltpu.VMEM((8, 2, 4, RADIX, 1024), BF16),
            pltpu.VMEM((8, GROUPS, HALF, GROUP, RADIX), BF16),
            pltpu.VMEM((2, GROUPS, HALF, GROUP, RADIX), BF16),
            pltpu.VMEM((HALF * 64, RADIX), F32),
            pltpu.VMEM((HALF // 2 * 64, RADIX), F32),
            pltpu.VMEM((4, HALF * GROUP, RADIX), F32),
            pltpu.VMEM((2, HALF * GROUP, RADIX), F32),
            pltpu.VMEM((2, 8, 64, 512), F32),
            pltpu.VMEM((2, 8, 64, 512), F32),
            square, square, square,
            dma((2,)), dma((2,)), dma((2,)), dma((4, 2)), dma((6,)), dma((8, 2, 2)), dma((32,)), dma((8, GROUPS)), dma((28,)),
            dma((2,)), dma((2, 2)), dma((2, 2)), dma((4,)), dma((4,)), dma((2,)),
        ],
        compiler_params=pltpu.CompilerParams(
            collective_id=0, has_side_effects=True, vmem_limit_bytes=60 << 20
        ),
        name="gradients",
    )(upstream, queries, keys, values, f, tokens, *tabs)


def body(tokens, queries, keys, values, upstream, filters):
    update, filter_half = gradients(upstream[0], queries[0], keys[0], values[0], filters.T, tokens[0])
    filter_grad = filter_half.T
    return (update[None] * 32.0, filter_grad)


def solution(mesh):
    return jax.shard_map(
        body,
        mesh=mesh,
        in_specs=(
            P("dp", "seq", None),
            P("dp", "seq", None),
            P("dp", "seq", None),
            P("dp", "seq", None),
            P("dp", "seq", None),
            P(None, "seq"),
        ),
        out_specs=(P("seq", None, "dp"), P("dp", "seq")),
        check_vma=False,
    )
```

```python
import math

import jax
import jax.numpy as jnp
import numpy as np
from jax import lax
from jax.experimental import pallas as pl
from jax.experimental.pallas import tpu as pltpu
from jax.sharding import PartitionSpec as P

F32, BF16 = jnp.float32, jnp.bfloat16
RADIX = 128
HALF = 64
NS_STEPS = 5
COEF_A = 3.4445
COEF_B = -4.775
COEF_C = 2.0315
ROWS = 72


def split_table(table):
    high = np.asarray(table, np.float32).astype(jnp.bfloat16)
    low = (np.asarray(table, np.float64) - high.astype(np.float64)).astype(jnp.bfloat16)
    return high, low


def fourier_tables():
    total = RADIX * RADIX
    spot = np.arange(RADIX)
    used = np.arange(HALF + 1)
    outer = 2.0 * math.pi * (np.outer(used, np.arange(HALF)) % RADIX) / RADIX
    first = np.zeros((2 * ROWS, HALF))
    first[: HALF + 1] = np.cos(outer)
    first[ROWS : ROWS + HALF + 1] = -np.sin(outer)
    weight = np.where((used == 0) | (used == HALF), 1.0, 2.0)[:, None] / total
    last = np.zeros((2 * ROWS, HALF))
    last[: HALF + 1] = np.cos(outer) * weight
    last[ROWS : ROWS + HALF + 1] = -np.sin(outer) * weight
    last = last.T
    inner = 2.0 * math.pi * (np.outer(spot, spot) % RADIX) / RADIX
    real, imag = np.cos(inner), -np.sin(inner)
    forward = np.block([[real, imag], [-imag, real]])
    turn = 2.0 * math.pi * np.outer(used, spot) / total
    twist = np.zeros((2, ROWS, RADIX), np.float32)
    twist[0, : HALF + 1] = np.cos(turn)
    twist[1, : HALF + 1] = -np.sin(turn)
    first_high, first_low = split_table(first)
    last_high, last_low = split_table(last)
    ahead_high, ahead_low = split_table(forward)
    back_high, back_low = split_table(forward.T)
    return (
        np.concatenate([first_high, first_low, first_high], 1),
        np.concatenate([ahead_high, ahead_high, ahead_low], 0),
        np.concatenate([back_high, back_high, back_low], 0),
        np.concatenate([last_high, last_low, last_high], 1),
        twist,
    )


def dot(left, right):
    return jnp.dot(left, right, preferred_element_type=F32)


def parts(value):
    high = value.astype(BF16)
    return high, (value - high.astype(F32)).astype(BF16)


def convolve_pair(grads, inputs, filters, tables):
    first_ref, ahead_ref, back_ref, last_ref, twist_ref = tables
    turn_real, turn_imag = twist_ref[0], twist_ref[1]
    signals = jnp.concatenate([grads[0], inputs[0], grads[1], inputs[1]], axis=1)
    signals = jnp.concatenate([signals, signals], axis=0)
    spread = dot(first_ref[:, : 2 * HALF], signals)
    high, low = parts(jnp.concatenate(filters, axis=1))
    spread_filter = dot(first_ref[...], jnp.concatenate([high, high, low], axis=0))
    turned = []
    for block in (spread, spread_filter):
        for at in range(0, block.shape[1], RADIX):
            real, imag = block[:ROWS, at : at + RADIX], block[ROWS:, at : at + RADIX]
            turned.append(
                jnp.concatenate(
                    [real * turn_real - imag * turn_imag, real * turn_imag + imag * turn_real], axis=1
                )
            )
    high, low = parts(jnp.concatenate(turned, axis=0))
    spectra = dot(jnp.concatenate([high, low, high], axis=1), ahead_ref[...])
    spec = [
        (spectra[i * ROWS : (i + 1) * ROWS, :RADIX], spectra[i * ROWS : (i + 1) * ROWS, RADIX:])
        for i in range(6)
    ]
    products = []
    for which in range(2):
        grad_real, grad_imag = spec[2 * which]
        input_real, input_imag = spec[2 * which + 1]
        filter_real, filter_imag = spec[4 + which]
        for other_real, other_imag, flip in (
            (filter_real, filter_imag, 0),
            (input_real, input_imag, 0),
        ):
            products.append(
                jnp.concatenate(
                    [
                        grad_real * other_real + grad_imag * other_imag,
                        grad_imag * other_real - grad_real * other_imag,
                    ],
                    axis=1,
                )
            )
    high, low = parts(jnp.concatenate(products, axis=0))
    mixed = dot(jnp.concatenate([high, low, high], axis=1), back_ref[...])
    columns = []
    for i in range(4):
        real, imag = mixed[i * ROWS : (i + 1) * ROWS, :RADIX], mixed[i * ROWS : (i + 1) * ROWS, RADIX:]
        columns.append(
            jnp.concatenate(
                [real * turn_real + imag * turn_imag, imag * turn_real - real * turn_imag], axis=0
            )
        )
    high, low = parts(jnp.concatenate(columns, axis=1))
    result = dot(last_ref[...], jnp.concatenate([high, high, low], axis=0))
    return [result[:, i * RADIX : (i + 1) * RADIX] for i in range(4)]


GROUP = 16


GROUPS = 4


def conv_group(at, stage, in_rows, fg_rows, out_rows, tables):
    def pair(j, carry):
        chans = [at + 2 * j, at + 2 * j + 1]
        spots = [pl.ds(2 * j + i, HALF, stride=GROUP) for i in range(2)]
        keys = [in_rows[1, spot, :] for spot in spots]
        values = [in_rows[2, spot, :] for spot in spots]
        inputs = [(a * b).astype(BF16) for a, b in zip(keys, values)]
        grads = [in_rows[0, spot, :].astype(BF16) for spot in spots]
        out = convolve_pair(grads, inputs, [in_rows[3, spot, :] for spot in spots], tables)
        for i in range(2):
            back = out[2 * i].astype(BF16).astype(F32)
            fg_rows[pl.ds(chans[i], HALF, stride=64), :] = out[2 * i + 1]
            out_rows[0, spots[i], :] = back * values[i]
            out_rows[1, spots[i], :] = back * keys[i]
        return carry

    lax.fori_loop(stage * GROUP // 4, (stage + 1) * GROUP // 4, pair, 0)


STRIDE = 37


def place():
    me = lax.axis_index("seq")
    return me // 32, me // 8 % 4, me // 2 % 4, me % 2


def seq_of(z, x, y, c):
    return ((z * 4 + x) * 4 + y) * 2 + c


def row_block(y, j):
    return y // 2, (y // 2 + j) % 2 * 2 + (y + y // 2) % 2


MESH = pl.DeviceIdType.MESH


def remote(src, dst, send, recv, **device):
    return pltpu.make_async_remote_copy(
        src_ref=src, dst_ref=dst, send_sem=send, recv_sem=recv, device_id=device, device_id_type=MESH
    )


def wait_bytes(ref, sem):
    pltpu.make_async_copy(ref, ref, sem).wait()


def product(left, right):
    left_high, left_low = parts(left)
    right_high, right_low = parts(right)
    left_side = jnp.concatenate([left_high, left_low, left_high], axis=1)
    right_side = jnp.concatenate([right_high, right_high, right_low], axis=0)
    return dot(left_side, right_side)


def gradient_kernel(
    up_ref, q_ref, k_ref, v_ref, f_ref, tok_ref, t0, t1, t2, t3, t4,
    update_ref, fg_ref,
    sent, got, tok, cols, own, fg_all, fg_in, in_rows, out_rows, part, landed, gram, gram_in, current,
    swap_send, swap_recv, swap_own, tok_first, tok_first_send, tok_recv, tok_send, col_recv, col_send,
    fg_sem, part_send, part_recv, gram_send, gram_recv, final_sem,
):
    tables = (t0, t1, t2, t3, t4)
    z, x, y, c = place()
    me = lax.axis_index("seq")
    dp = lax.axis_index("dp")
    n_seq = lax.axis_size("seq")
    up, down, across = (y + 1) % 4, (y + 3) % 4, (y + 2) % 4
    right, left, far = (x + 1) % 4, (x + 3) % 4, (x + 2) % 4
    sibling = seq_of(z, x, y, 1 - c)
    x_right, x_left = seq_of(z, right, y, c), seq_of(z, left, y, c)
    z_other = seq_of(1 - z, x, y, c)
    mine = (x + y + x // 2) % 2
    kind = (dp + x + y + y // 2) % 2
    side_here = (c + dp) % 2
    finish_x = [x // 2 * 2 + (j + y + x // 2) % 2 for j in range(2)]
    finish_dp = [(c + finish_x[j] + y + y // 2) % 2 for j in range(2)]
    finish_seq = [seq_of(z, finish_x[j], y, (x + finish_dp[j]) % 2) for j in range(2)]
    source_seq = seq_of(z, x // 2 * 2 + side_here, y, kind)
    owner_z, owner_x = row_block(y, mine)
    owner = seq_of(owner_z, owner_x, 2 * kind + z, x // 2)
    owner_dp = side_here
    maker_y = 2 * z + (x + z) % 2
    maker_x = 2 * c + (x // 2 + z + maker_y + c) % 2
    maker_dp = (y // 2 + maker_x + maker_y + z) % 2
    maker = seq_of(y % 2, maker_x, maker_y, (dp + maker_dp) % 2)

    barrier = pltpu.get_barrier_semaphore()

    def greet(d, carry):
        pl.semaphore_signal(barrier, inc=1, device_id={"seq": (me + d) % n_seq}, device_id_type=MESH)
        return carry

    lax.fori_loop(1, n_seq, greet, 0)
    pl.semaphore_signal(barrier, inc=1, device_id={"dp": 1 - dp}, device_id_type=MESH)

    pl.semaphore_signal(barrier, inc=1, device_id={"seq": source_seq, "dp": 1 - dp}, device_id_type=MESH)

    @pl.when(maker_dp != dp)
    def _():
        pl.semaphore_signal(barrier, inc=1, device_id={"seq": maker, "dp": 1 - dp}, device_id_type=MESH)

    pl.semaphore_wait(barrier, n_seq + 1 + (owner_dp + dp) % 2)

    def swap_piece(peer, group_at):
        return remote(
            sent.at[peer, group_at], got.at[group_at, me], swap_send.at[group_at], swap_recv.at[group_at], seq=peer
        )

    def swap_here(group_at):
        return pltpu.make_async_copy(sent.at[me, group_at], got.at[group_at, me], swap_own.at[group_at])

    def prepare(chip):
        span = pl.ds(pl.multiple_of(chip * RADIX, RADIX), RADIX)
        conv_grad = up_ref[:, span].astype(F32) * q_ref[:, span].astype(F32)
        for kind, item in enumerate((conv_grad, k_ref[:, span].astype(F32), v_ref[:, span].astype(F32))):
            turned = item.T.astype(BF16)
            for core in range(2):
                for i in range(GROUPS):
                    at = 64 * core + GROUP * i
                    sent[2 * chip + core, i, kind] = turned[at : at + GROUP]

    def first_group(i, carry):
        chip = (me // 2 + 19 * i) % (n_seq // 2)
        prepare(chip)
        for core in range(2):
            swap_piece(2 * chip + core, 0).start()
        return carry

    def swap_group(i):
        def one(d, carry):
            swap_piece((me + STRIDE * d) % n_seq, i).start()
            return carry

        lax.fori_loop(1, n_seq, one, 0)

    def wait_swap(group_at):
        wait_bytes(got.at[group_at, pl.ds(0, 63)], swap_recv.at[group_at])
        wait_bytes(got.at[group_at, 0], swap_own.at[group_at])

    prepare(me // 2)
    swap_piece(sibling, 0).start()
    for i in range(GROUPS):
        swap_here(i).start()
    lax.fori_loop(1, n_seq // 2, first_group, 0)

    pending = []

    def launch(copy):
        copy.start()
        pending.append(copy)

    here = z * 4 + x

    def quarter(at, j):
        block_z, block_x = row_block(at, j)
        return tok_ref.at[:, pl.ds(pl.multiple_of((block_z * 4 + block_x) * 512, 512), 512)]

    def spot(j):
        return tok.at[here, c, y, :, pl.ds(512 * j, 512)]

    for j in range(2):
        for i, target in enumerate((up, down, across)):
            launch(
                remote(
                    quarter(target, j), spot(j), tok_first_send.at[2 * i + j], tok_first.at[i, j],
                    seq=seq_of(z, x, target, c),
                )
            )
        pltpu.make_async_copy(quarter(y, j), spot(j), tok_first.at[3, j]).start()
    swap_group(1)

    count = [0]

    def half(zz, xx, cc, h):
        return tok.at[zz * 4 + xx, cc, pl.ds(2 * h, 2)]

    def send_half(zz, xx, h, target):
        launch(
            remote(
                half(zz, xx, c, h), half(zz, xx, c, h), tok_send.at[count[0]],
                tok_recv.at[zz * 4 + xx, c, h], seq=target,
            )
        )
        count[0] += 1

    def wait_half(zz, xx, cc, h):
        wait_bytes(half(zz, xx, cc, h), tok_recv.at[zz * 4 + xx, cc, h])

    def wait_first():
        for i, source_y in ((0, down), (1, up), (2, across), (3, y)):
            for j in range(2):
                wait_bytes(tok.at[here, c, source_y, :, pl.ds(512 * j, 512)], tok_first.at[i, j])

    def spread(zz):
        for a, b in ((0, 1), (1, 0)):
            send_half(zz, x, a, x_right)
            send_half(zz, x, b, x_left)

    def relay(zz):
        wait_half(zz, left, c, 0)
        send_half(zz, left, 0, x_right)
        wait_half(zz, right, c, 1)
        send_half(zz, right, 1, x_left)

    def share(zz, xx, h):
        send_half(zz, xx, h, sibling)

    def slot(yy, cc, i):
        return (yy * 2 + cc, i)

    def send_group(i):
        mine = cols.at[slot(y, c, i)]
        arrival = col_recv.at[slot(y, c, i)]
        for n, (kind, target) in enumerate(((0, up), (1, up), (0, down), (1, down))):
            launch(
                remote(own.at[kind, i], mine, col_send.at[i * 5 + n], arrival, seq=seq_of(z, x, target, kind))
            )
        launch(remote(own.at[1 - c, i], mine, col_send.at[i * 5 + 4], arrival, seq=sibling))
        pltpu.make_async_copy(own.at[c, i], mine, arrival).start()

    def wait_col(at):
        wait_bytes(cols.at[at], col_recv.at[at])

    forwarded = [0]

    def relay_group(i):
        source_y, target = (down, up) if i % 2 == 0 else (up, down)
        for cc in range(2):
            at = slot(source_y, cc, i)
            wait_col(at)
            launch(
                remote(
                    cols.at[at], cols.at[at], col_send.at[5 * GROUPS + forwarded[0]], col_recv.at[at],
                    seq=seq_of(z, x, target, c),
                )
            )
            forwarded[0] += 1

    def compute(i, stage):
        if stage == 0:
            for kind in range(3):
                chunk = got[i, :, kind]
                in_rows[kind] = chunk.astype(F32).reshape(HALF * GROUP, RADIX)
            for n in range(HALF):
                in_rows[3, GROUP * n : GROUP * (n + 1), :] = f_ref[
                    GROUP * i : GROUP * (i + 1), RADIX * n : RADIX * (n + 1)
                ]
        conv_group(i * GROUP, stage, in_rows, fg_all, out_rows, tables)
        if stage == 1:
            for kind in range(2):
                own[kind, i] = out_rows[kind].reshape(HALF, GROUP, RADIX).astype(BF16)
            send_group(i)

    wait_swap(0)
    compute(0, 0)
    swap_group(2)
    swap_group(3)
    wait_first()
    spread(z)
    for h in range(2):
        send_half(z, x, h, z_other)
        share(z, x, h)
    compute(0, 1)
    wait_swap(1)
    compute(1, 0)
    relay(z)
    compute(1, 1)
    wait_swap(2)
    relay_group(0)
    compute(2, 0)
    for h in range(2):
        wait_half(1 - z, x, c, h)
    spread(1 - z)
    for xx, h in ((left, 0), (right, 1)):
        share(z, xx, h)
    compute(2, 1)
    relay_group(1)
    for xx, h in ((left, 1), (right, 0)):
        wait_half(z, xx, c, h)
        share(z, xx, h)
    for h in range(2):
        share(1 - z, x, h)
    wait_swap(3)
    compute(3, 0)
    for h in range(2):
        wait_half(z, far, c, h)
        share(z, far, h)
    relay(1 - z)
    compute(3, 1)
    fg_copy = remote(
        fg_all.at[pl.ds(pl.multiple_of((1 - dp) * 2048, 2048), 2048)], fg_in, fg_sem.at[0], fg_sem.at[1], dp=1 - dp
    )
    launch(fg_copy)
    def wait_group(i):
        for cc in range(2):
            wait_col(slot(y, cc, i))
            wait_col(slot(across, cc, i))
            wait_col(slot(up if i % 2 == 0 else down, cc, i))

    def multiply(zx, side, fresh):
        left_side = jnp.concatenate(
            [
                cols[:, pl.ds(2 * side, 2), zx * 8 + yy * 2 + cc].reshape(256, RADIX)
                for cc in range(2)
                for yy in range(4)
            ],
            axis=1,
        )

        def tile(n, carry):
            j, at = n // 2, pl.multiple_of(n % 2 * 256, 256)
            right_side = tok[zx, :, :, :, pl.ds(pl.multiple_of(n * 256, 256), 256)].reshape(1024, 256)
            term = dot(left_side, right_side).reshape(8, 32, 256)
            if fresh:
                part[j, :, pl.ds(32 * side, 32), pl.ds(at, 256)] = term
            else:
                part[j, :, pl.ds(32 * side, 32), pl.ds(at, 256)] += term
            return carry

        lax.fori_loop(0, 4, tile, 0)

    stays = [jnp.logical_and(finish_seq[j] == me, finish_dp[j] == dp) for j in range(2)]

    def part_copy(j, side):
        view = (slice(None), pl.ds(32 * side, 32))
        src, dst, arrival = part.at[(j, *view)], landed.at[(dp, *view)], part_recv.at[dp, side]
        return (
            remote(src, dst, part_send.at[j, side], arrival, seq=finish_seq[j], dp=finish_dp[j]),
            pltpu.make_async_copy(src, dst, arrival),
        )

    def send_parts(side):
        for j in range(2):
            away, at_home = part_copy(j, side)

            @pl.when(stays[j])
            def _():
                at_home.start()

            @pl.when(jnp.logical_not(stays[j]))
            def _():
                away.start()

    def multiply_all(zz, side, fresh):
        if fresh:
            multiply(zz * 4 + x, side, True)

        def more(i, carry):
            multiply(zz * 4 + (x + i) % 4, side, False)
            return carry

        lax.fori_loop(1 if fresh else 0, 4, more, 0)

    def wait_tokens(zz):
        for xx in (x, left, right, far):
            for h in range(2):
                wait_half(zz, xx, 1 - c, h)

    relay_group(2)
    wait_group(0)
    wait_group(1)
    wait_tokens(z)
    multiply_all(z, 0, True)
    for xx, h in ((left, 0), (right, 1)):
        share(1 - z, xx, h)
    for xx, h in ((left, 1), (right, 0)):
        wait_half(1 - z, xx, c, h)
        share(1 - z, xx, h)
    relay_group(3)
    for h in range(2):
        wait_half(1 - z, far, c, h)
        share(1 - z, far, h)
    wait_tokens(1 - z)
    multiply_all(1 - z, 0, False)
    send_parts(0)
    wait_group(2)
    wait_group(3)
    multiply_all(z, 1, True)
    multiply_all(1 - z, 1, False)
    send_parts(1)
    fg_copy.wait_recv()
    for n in range(HALF // 2):
        kept = fg_all[pl.ds(pl.multiple_of(dp * 2048 + 64 * n, 64), 64), :]
        fg_ref[:, RADIX * n : RADIX * (n + 1)] = kept + fg_in[64 * n : 64 * (n + 1), :]

    for side in range(2):
        for d in range(2):
            wait_bytes(landed.at[d, :, pl.ds(32 * side, 32)], part_recv.at[d, side])
        columns = landed[0, :, pl.ds(32 * side, 32), :] + landed[1, :, pl.ds(32 * side, 32), :]
        columns = columns.reshape(256, 512)
        term = product(columns.T, columns)
        if side == 0:
            gram[...] = term
        else:
            gram[...] += term
    exchanges = []
    for i in range(4):
        view = (pl.ds(128 * i, 128), pl.ds(128 * i, 512 - 128 * i))
        copy = remote(gram.at[view], gram_in.at[view], gram_send.at[i], gram_recv.at[i], seq=sibling)
        launch(copy)
        exchanges.append(copy)
    current[...] = (landed[0] + landed[1]).reshape(512, 512).T
    for copy in exchanges:
        copy.wait_recv()
    diagonal = lax.broadcasted_iota(jnp.int32, (128, 128), 0) == lax.broadcasted_iota(jnp.int32, (128, 128), 1)
    trace = jnp.zeros((1, 1), F32)
    for i in range(4):
        block = gram[128 * i : 128 * (i + 1), 128 * i : 128 * (i + 1)]
        block = block + gram_in[128 * i : 128 * (i + 1), 128 * i : 128 * (i + 1)]
        trace = trace + jnp.sum(jnp.where(diagonal, block, 0.0), keepdims=True)
    scale = 1.0 / (jnp.sqrt(trace) + 1e-07)
    for i in range(4):
        for j in range(i, 4):
            at = (slice(128 * i, 128 * (i + 1)), slice(128 * j, 128 * (j + 1)))
            block = (gram[at] + gram_in[at]) * scale * scale
            gram_in[at] = block
            if j > i:
                gram_in[at[1], at[0]] = block.T
    current[...] = current[...] * scale

    def step(i, carry):
        gram_now = gram_in[...]
        mixer = COEF_B * gram_now + COEF_C * product(gram_now, gram_now)
        current[...] = COEF_A * current[...] + product(mixer, current[...])
        half_step = COEF_A * gram_now + product(mixer, gram_now)
        gram_in[...] = COEF_A * half_step + product(half_step, mixer)
        return carry

    lax.fori_loop(0, NS_STEPS - 1, step, 0)
    gram_now = gram_in[...]
    mixer = COEF_B * gram_now + COEF_C * product(gram_now, gram_now)
    current[...] = COEF_A * current[...] + product(mixer, current[...])
    is_owner = jnp.logical_and(owner == me, owner_dp == dp)
    away = remote(current, update_ref, final_sem.at[0], final_sem.at[1], seq=owner, dp=owner_dp)

    @pl.when(is_owner)
    def _():
        pltpu.make_async_copy(current, update_ref, final_sem.at[1]).start()

    @pl.when(jnp.logical_not(is_owner))
    def _():
        away.start()

    wait_bytes(update_ref, final_sem.at[1])

    @pl.when(jnp.logical_not(is_owner))
    def _():
        away.wait_send()

    for side in range(2):
        for j in range(2):
            away, _ = part_copy(j, side)

            @pl.when(jnp.logical_not(stays[j]))
            def _():
                away.wait_send()

    for i in range(GROUPS):
        wait_bytes(got.at[i, pl.ds(0, 63)], swap_send.at[i])
    for copy in pending:
        copy.wait_send()


def gradients(upstream, queries, keys, values, f, tokens):
    tabs = [jnp.asarray(t) for t in fourier_tables()]
    vm = pl.BlockSpec(memory_space=pltpu.VMEM)
    dma = pltpu.SemaphoreType.DMA
    square = pltpu.VMEM((512, 512), F32)
    return pl.pallas_call(
        gradient_kernel,
        out_shape=(
            jax.ShapeDtypeStruct((512, 512), F32),
            jax.ShapeDtypeStruct((64, HALF // 2 * RADIX), F32),
        ),
        in_specs=[vm] * 11,
        out_specs=[vm] * 2,
        scratch_shapes=[
            pltpu.VMEM((64, GROUPS, 3, GROUP, RADIX), BF16),
            pltpu.VMEM((GROUPS, 64, 3, GROUP, RADIX), BF16),
            pltpu.VMEM((8, 2, 4, RADIX, 1024), BF16),
            pltpu.VMEM((8, GROUPS, HALF, GROUP, RADIX), BF16),
            pltpu.VMEM((2, GROUPS, HALF, GROUP, RADIX), BF16),
            pltpu.VMEM((HALF * 64, RADIX), F32),
            pltpu.VMEM((HALF // 2 * 64, RADIX), F32),
            pltpu.VMEM((4, HALF * GROUP, RADIX), F32),
            pltpu.VMEM((2, HALF * GROUP, RADIX), F32),
            pltpu.VMEM((2, 8, 64, 512), F32),
            pltpu.VMEM((2, 8, 64, 512), F32),
            square, square, square,
            dma((GROUPS,)), dma((GROUPS,)), dma((GROUPS,)), dma((4, 2)), dma((6,)), dma((8, 2, 2)), dma((32,)), dma((8, GROUPS)), dma((28,)),
            dma((2,)), dma((2, 2)), dma((2, 2)), dma((4,)), dma((4,)), dma((2,)),
        ],
        compiler_params=pltpu.CompilerParams(
            collective_id=0, has_side_effects=True, vmem_limit_bytes=60 << 20
        ),
        name="gradients",
    )(upstream, queries, keys, values, f, tokens, *tabs)


def body(tokens, queries, keys, values, upstream, filters):
    update, filter_half = gradients(upstream[0], queries[0], keys[0], values[0], filters.T, tokens[0])
    filter_grad = filter_half.T
    return (update[None] * 32.0, filter_grad)


def solution(mesh):
    return jax.shard_map(
        body,
        mesh=mesh,
        in_specs=(
            P("dp", "seq", None),
            P("dp", "seq", None),
            P("dp", "seq", None),
            P("dp", "seq", None),
            P("dp", "seq", None),
            P(None, "seq"),
        ),
        out_specs=(P("seq", None, "dp"), P("dp", "seq")),
        check_vma=False,
    )
```

```python
import math

import jax
import jax.numpy as jnp
import numpy as np
from jax import lax
from jax.experimental import pallas as pl
from jax.experimental.pallas import tpu as pltpu
from jax.sharding import PartitionSpec as P

F32, BF16 = jnp.float32, jnp.bfloat16
RADIX = 128
HALF = 64
NS_STEPS = 5
COEF_A = 3.4445
COEF_B = -4.775
COEF_C = 2.0315
ROWS = 72


def split_table(table):
    high = np.asarray(table, np.float32).astype(jnp.bfloat16)
    low = (np.asarray(table, np.float64) - high.astype(np.float64)).astype(jnp.bfloat16)
    return high, low


def fourier_tables():
    total = RADIX * RADIX
    spot = np.arange(RADIX)
    used = np.arange(HALF + 1)
    outer = 2.0 * math.pi * (np.outer(used, np.arange(HALF)) % RADIX) / RADIX
    first = np.zeros((2 * ROWS, HALF))
    first[: HALF + 1] = np.cos(outer)
    first[ROWS : ROWS + HALF + 1] = -np.sin(outer)
    weight = np.where((used == 0) | (used == HALF), 1.0, 2.0)[:, None] / total
    last = np.zeros((2 * ROWS, HALF))
    last[: HALF + 1] = np.cos(outer) * weight
    last[ROWS : ROWS + HALF + 1] = -np.sin(outer) * weight
    last = last.T
    inner = 2.0 * math.pi * (np.outer(spot, spot) % RADIX) / RADIX
    real, imag = np.cos(inner), -np.sin(inner)
    forward = np.block([[real, imag], [-imag, real]])
    turn = 2.0 * math.pi * np.outer(used, spot) / total
    twist = np.zeros((2, ROWS, RADIX), np.float32)
    twist[0, : HALF + 1] = np.cos(turn)
    twist[1, : HALF + 1] = -np.sin(turn)
    first_high, first_low = split_table(first)
    last_high, last_low = split_table(last)
    ahead_high, ahead_low = split_table(forward)
    back_high, back_low = split_table(forward.T)
    return (
        np.concatenate([first_high, first_low, first_high], 1),
        np.concatenate([ahead_high, ahead_high, ahead_low], 0),
        np.concatenate([back_high, back_high, back_low], 0),
        np.concatenate([last_high, last_low, last_high], 1),
        twist,
    )


def dot(left, right):
    return jnp.dot(left, right, preferred_element_type=F32)


def parts(value):
    high = value.astype(BF16)
    return high, (value - high.astype(F32)).astype(BF16)


def convolve_pair(grads, inputs, filters, tables):
    first_ref, ahead_ref, back_ref, last_ref, twist_ref = tables
    turn_real, turn_imag = twist_ref[0], twist_ref[1]
    signals = jnp.concatenate([grads[0], inputs[0], grads[1], inputs[1]], axis=1)
    signals = jnp.concatenate([signals, signals], axis=0)
    spread = dot(first_ref[:, : 2 * HALF], signals)
    high, low = parts(jnp.concatenate(filters, axis=1))
    spread_filter = dot(first_ref[...], jnp.concatenate([high, high, low], axis=0))
    turned = []
    for block in (spread, spread_filter):
        for at in range(0, block.shape[1], RADIX):
            real, imag = block[:ROWS, at : at + RADIX], block[ROWS:, at : at + RADIX]
            turned.append(
                jnp.concatenate(
                    [real * turn_real - imag * turn_imag, real * turn_imag + imag * turn_real], axis=1
                )
            )
    high, low = parts(jnp.concatenate(turned, axis=0))
    spectra = dot(jnp.concatenate([high, low, high], axis=1), ahead_ref[...])
    spec = [
        (spectra[i * ROWS : (i + 1) * ROWS, :RADIX], spectra[i * ROWS : (i + 1) * ROWS, RADIX:])
        for i in range(6)
    ]
    products = []
    for which in range(2):
        grad_real, grad_imag = spec[2 * which]
        input_real, input_imag = spec[2 * which + 1]
        filter_real, filter_imag = spec[4 + which]
        for other_real, other_imag, flip in (
            (filter_real, filter_imag, 0),
            (input_real, input_imag, 0),
        ):
            products.append(
                jnp.concatenate(
                    [
                        grad_real * other_real + grad_imag * other_imag,
                        grad_imag * other_real - grad_real * other_imag,
                    ],
                    axis=1,
                )
            )
    high, low = parts(jnp.concatenate(products, axis=0))
    mixed = dot(jnp.concatenate([high, low, high], axis=1), back_ref[...])
    columns = []
    for i in range(4):
        real, imag = mixed[i * ROWS : (i + 1) * ROWS, :RADIX], mixed[i * ROWS : (i + 1) * ROWS, RADIX:]
        columns.append(
            jnp.concatenate(
                [real * turn_real + imag * turn_imag, imag * turn_real - real * turn_imag], axis=0
            )
        )
    high, low = parts(jnp.concatenate(columns, axis=1))
    result = dot(last_ref[...], jnp.concatenate([high, high, low], axis=0))
    return [result[:, i * RADIX : (i + 1) * RADIX] for i in range(4)]


GROUP = 16


GROUPS = 4


def conv_group(at, stage, in_rows, fg_rows, out_rows, tables):
    def pair(j, carry):
        chans = [at + 2 * j, at + 2 * j + 1]
        spots = [pl.ds(2 * j + i, HALF, stride=GROUP) for i in range(2)]
        keys = [in_rows[1, spot, :] for spot in spots]
        values = [in_rows[2, spot, :] for spot in spots]
        inputs = [(a * b).astype(BF16) for a, b in zip(keys, values)]
        grads = [in_rows[0, spot, :].astype(BF16) for spot in spots]
        out = convolve_pair(grads, inputs, [in_rows[3, spot, :] for spot in spots], tables)
        for i in range(2):
            back = out[2 * i].astype(BF16).astype(F32)
            fg_rows[pl.ds(chans[i], HALF, stride=64), :] = out[2 * i + 1]
            out_rows[0, spots[i], :] = back * values[i]
            out_rows[1, spots[i], :] = back * keys[i]
        return carry

    lax.fori_loop(stage * GROUP // 4, (stage + 1) * GROUP // 4, pair, 0)


STRIDE = 37


def place():
    me = lax.axis_index("seq")
    return me // 32, me // 8 % 4, me // 2 % 4, me % 2


def seq_of(z, x, y, c):
    return ((z * 4 + x) * 4 + y) * 2 + c


def row_block(y, j):
    return y // 2, (y // 2 + j) % 2 * 2 + (y + y // 2) % 2


MESH = pl.DeviceIdType.MESH


def remote(src, dst, send, recv, **device):
    return pltpu.make_async_remote_copy(
        src_ref=src, dst_ref=dst, send_sem=send, recv_sem=recv, device_id=device, device_id_type=MESH
    )


def wait_bytes(ref, sem):
    pltpu.make_async_copy(ref, ref, sem).wait()


def product(left, right):
    left_high, left_low = parts(left)
    right_high, right_low = parts(right)
    left_side = jnp.concatenate([left_high, left_low, left_high], axis=1)
    right_side = jnp.concatenate([right_high, right_high, right_low], axis=0)
    return dot(left_side, right_side)


def gradient_kernel(
    up_ref, q_ref, k_ref, v_ref, f_ref, tok_ref, t0, t1, t2, t3, t4,
    update_ref, fg_ref,
    sent, got, tok, cols, own, fg_all, fg_in, in_rows, out_rows, part, landed, gram, gram_in, current,
    swap_send, swap_recv, swap_own, tok_first, tok_first_send, tok_recv, tok_send, col_recv, col_send,
    fg_sem, part_send, part_recv, gram_send, gram_recv, final_sem,
):
    tables = (t0, t1, t2, t3, t4)
    z, x, y, c = place()
    me = lax.axis_index("seq")
    dp = lax.axis_index("dp")
    n_seq = lax.axis_size("seq")
    up, down, across = (y + 1) % 4, (y + 3) % 4, (y + 2) % 4
    right, left, far = (x + 1) % 4, (x + 3) % 4, (x + 2) % 4
    sibling = seq_of(z, x, y, 1 - c)
    x_right, x_left = seq_of(z, right, y, c), seq_of(z, left, y, c)
    z_other = seq_of(1 - z, x, y, c)
    mine = (x + y + x // 2) % 2
    kind = (dp + x + y + y // 2) % 2
    side_here = (c + dp) % 2
    finish_x = [x // 2 * 2 + (j + y + x // 2) % 2 for j in range(2)]
    finish_dp = [(c + finish_x[j] + y + y // 2) % 2 for j in range(2)]
    finish_seq = [seq_of(z, finish_x[j], y, (x + finish_dp[j]) % 2) for j in range(2)]
    source_seq = seq_of(z, x // 2 * 2 + side_here, y, kind)
    owner_z, owner_x = row_block(y, mine)
    owner = seq_of(owner_z, owner_x, 2 * kind + z, x // 2)
    owner_dp = side_here
    maker_y = 2 * z + (x + z) % 2
    maker_x = 2 * c + (x // 2 + z + maker_y + c) % 2
    maker_dp = (y // 2 + maker_x + maker_y + z) % 2
    maker = seq_of(y % 2, maker_x, maker_y, (dp + maker_dp) % 2)

    barrier = pltpu.get_barrier_semaphore()

    def greet(d, carry):
        pl.semaphore_signal(barrier, inc=1, device_id={"seq": (me + d) % n_seq}, device_id_type=MESH)
        return carry

    lax.fori_loop(1, n_seq, greet, 0)
    pl.semaphore_signal(barrier, inc=1, device_id={"dp": 1 - dp}, device_id_type=MESH)

    pl.semaphore_signal(barrier, inc=1, device_id={"seq": source_seq, "dp": 1 - dp}, device_id_type=MESH)

    @pl.when(maker_dp != dp)
    def _():
        pl.semaphore_signal(barrier, inc=1, device_id={"seq": maker, "dp": 1 - dp}, device_id_type=MESH)

    pl.semaphore_wait(barrier, n_seq + 1 + (owner_dp + dp) % 2)

    def swap_piece(peer, group_at):
        return remote(
            sent.at[peer, group_at], got.at[group_at, me], swap_send.at[group_at], swap_recv.at[group_at], seq=peer
        )

    def swap_here(group_at):
        return pltpu.make_async_copy(sent.at[me, group_at], got.at[group_at, me], swap_own.at[group_at])

    def prepare(chip):
        span = pl.ds(pl.multiple_of(chip * RADIX, RADIX), RADIX)
        conv_grad = up_ref[:, span].astype(F32) * q_ref[:, span].astype(F32)
        for kind, item in enumerate((conv_grad, k_ref[:, span].astype(F32), v_ref[:, span].astype(F32))):
            turned = item.T.astype(BF16)
            for core in range(2):
                for i in range(GROUPS):
                    at = 64 * core + GROUP * i
                    sent[2 * chip + core, i, kind] = turned[at : at + GROUP]

    def first_group(i, carry):
        chip = (me // 2 + 19 * i) % (n_seq // 2)
        prepare(chip)
        for core in range(2):
            swap_piece(2 * chip + core, 0).start()
        return carry

    def swap_group(i):
        def one(d, carry):
            swap_piece((me + STRIDE * d) % n_seq, i).start()
            return carry

        lax.fori_loop(1, n_seq, one, 0)

    def wait_swap(group_at):
        wait_bytes(got.at[group_at, pl.ds(0, 63)], swap_recv.at[group_at])
        wait_bytes(got.at[group_at, 0], swap_own.at[group_at])

    prepare(me // 2)
    swap_piece(sibling, 0).start()
    for i in range(GROUPS):
        swap_here(i).start()
    lax.fori_loop(1, n_seq // 2, first_group, 0)

    pending = []

    def launch(copy):
        copy.start()
        pending.append(copy)

    here = z * 4 + x

    def quarter(at, j):
        block_z, block_x = row_block(at, j)
        return tok_ref.at[:, pl.ds(pl.multiple_of((block_z * 4 + block_x) * 512, 512), 512)]

    def spot(j):
        return tok.at[here, c, y, :, pl.ds(512 * j, 512)]

    for j in range(2):
        for i, target in enumerate((up, down, across)):
            launch(
                remote(
                    quarter(target, j), spot(j), tok_first_send.at[2 * i + j], tok_first.at[i, j],
                    seq=seq_of(z, x, target, c),
                )
            )
        pltpu.make_async_copy(quarter(y, j), spot(j), tok_first.at[3, j]).start()
    swap_group(1)

    count = [0]

    def half(zz, xx, cc, h):
        return tok.at[zz * 4 + xx, cc, pl.ds(2 * h, 2)]

    def send_half(zz, xx, h, target):
        launch(
            remote(
                half(zz, xx, c, h), half(zz, xx, c, h), tok_send.at[count[0]],
                tok_recv.at[zz * 4 + xx, c, h], seq=target,
            )
        )
        count[0] += 1

    def wait_half(zz, xx, cc, h):
        wait_bytes(half(zz, xx, cc, h), tok_recv.at[zz * 4 + xx, cc, h])

    def wait_first():
        for i, source_y in ((0, down), (1, up), (2, across), (3, y)):
            for j in range(2):
                wait_bytes(tok.at[here, c, source_y, :, pl.ds(512 * j, 512)], tok_first.at[i, j])

    def spread(zz):
        for a, b in ((0, 1), (1, 0)):
            send_half(zz, x, a, x_right)
            send_half(zz, x, b, x_left)

    def relay(zz):
        wait_half(zz, left, c, 0)
        send_half(zz, left, 0, x_right)
        wait_half(zz, right, c, 1)
        send_half(zz, right, 1, x_left)

    def share(zz, xx, h):
        send_half(zz, xx, h, sibling)

    def slot(yy, cc, i):
        return (yy * 2 + cc, i)

    def send_group(i):
        mine = cols.at[slot(y, c, i)]
        arrival = col_recv.at[slot(y, c, i)]
        for n, (kind, target) in enumerate(((0, up), (1, up), (0, down), (1, down))):
            launch(
                remote(own.at[kind, i], mine, col_send.at[i * 5 + n], arrival, seq=seq_of(z, x, target, kind))
            )
        launch(remote(own.at[1 - c, i], mine, col_send.at[i * 5 + 4], arrival, seq=sibling))
        pltpu.make_async_copy(own.at[c, i], mine, arrival).start()

    def wait_col(at):
        wait_bytes(cols.at[at], col_recv.at[at])

    forwarded = [0]

    def relay_group(i):
        source_y, target = (down, up) if i % 2 == 0 else (up, down)
        for cc in range(2):
            at = slot(source_y, cc, i)
            wait_col(at)
            launch(
                remote(
                    cols.at[at], cols.at[at], col_send.at[5 * GROUPS + forwarded[0]], col_recv.at[at],
                    seq=seq_of(z, x, target, c),
                )
            )
            forwarded[0] += 1

    def compute(i, stage):
        if stage == 0:
            for kind in range(3):
                chunk = got[i, :, kind]
                in_rows[kind] = chunk.astype(F32).reshape(HALF * GROUP, RADIX)
            for n in range(HALF):
                in_rows[3, GROUP * n : GROUP * (n + 1), :] = f_ref[
                    GROUP * i : GROUP * (i + 1), RADIX * n : RADIX * (n + 1)
                ]
        conv_group(i * GROUP, stage, in_rows, fg_all, out_rows, tables)
        if stage == 1:
            for kind in range(2):
                own[kind, i] = out_rows[kind].reshape(HALF, GROUP, RADIX).astype(BF16)
            send_group(i)

    wait_swap(0)
    compute(0, 0)
    swap_group(2)
    swap_group(3)
    wait_first()
    spread(z)
    for h in range(2):
        send_half(z, x, h, z_other)
        share(z, x, h)
    compute(0, 1)
    wait_swap(1)
    compute(1, 0)
    relay(z)
    compute(1, 1)
    wait_swap(2)
    relay_group(0)
    compute(2, 0)
    for h in range(2):
        wait_half(1 - z, x, c, h)
    spread(1 - z)
    for xx, h in ((left, 0), (right, 1)):
        share(z, xx, h)
    compute(2, 1)
    relay_group(1)
    for xx, h in ((left, 1), (right, 0)):
        wait_half(z, xx, c, h)
        share(z, xx, h)
    for h in range(2):
        share(1 - z, x, h)
    wait_swap(3)
    compute(3, 0)
    for h in range(2):
        wait_half(z, far, c, h)
        share(z, far, h)
    relay(1 - z)
    compute(3, 1)
    fg_copy = remote(
        fg_all.at[pl.ds(pl.multiple_of((1 - dp) * 2048, 2048), 2048)], fg_in, fg_sem.at[0], fg_sem.at[1], dp=1 - dp
    )
    launch(fg_copy)
    def wait_group(i):
        for cc in range(2):
            wait_col(slot(y, cc, i))
            wait_col(slot(across, cc, i))
            wait_col(slot(up if i % 2 == 0 else down, cc, i))

    def multiply(zx, side, fresh):
        left_side = jnp.concatenate(
            [
                cols[:, pl.ds(2 * side, 2), zx * 8 + yy * 2 + cc].reshape(256, RADIX)
                for cc in range(2)
                for yy in range(4)
            ],
            axis=1,
        )

        def tile(n, carry):
            j, at = n // 2, pl.multiple_of(n % 2 * 256, 256)
            right_side = tok[zx, :, :, :, pl.ds(pl.multiple_of(n * 256, 256), 256)].reshape(1024, 256)
            term = dot(left_side, right_side).reshape(8, 32, 256)
            if fresh:
                part[j, :, pl.ds(32 * side, 32), pl.ds(at, 256)] = term
            else:
                part[j, :, pl.ds(32 * side, 32), pl.ds(at, 256)] += term
            return carry

        lax.fori_loop(0, 4, tile, 0)

    stays = [jnp.logical_and(finish_seq[j] == me, finish_dp[j] == dp) for j in range(2)]

    def part_copy(j, side):
        view = (slice(None), pl.ds(32 * side, 32))
        src, dst, arrival = part.at[(j, *view)], landed.at[(dp, *view)], part_recv.at[dp, side]
        return (
            remote(src, dst, part_send.at[j, side], arrival, seq=finish_seq[j], dp=finish_dp[j]),
            pltpu.make_async_copy(src, dst, arrival),
        )

    def send_parts(side):
        for j in range(2):
            away, at_home = part_copy(j, side)

            @pl.when(stays[j])
            def _():
                at_home.start()

            @pl.when(jnp.logical_not(stays[j]))
            def _():
                away.start()

    def multiply_all(zz, side, fresh):
        if fresh:
            multiply(zz * 4 + x, side, True)

        def more(i, carry):
            multiply(zz * 4 + (x + i) % 4, side, False)
            return carry

        lax.fori_loop(1 if fresh else 0, 4, more, 0)

    def wait_tokens(zz):
        for xx in (x, left, right, far):
            for h in range(2):
                wait_half(zz, xx, 1 - c, h)

    relay_group(2)
    wait_group(0)
    wait_group(1)
    wait_tokens(z)
    multiply_all(z, 0, True)
    for xx, h in ((left, 0), (right, 1)):
        share(1 - z, xx, h)
    for xx, h in ((left, 1), (right, 0)):
        wait_half(1 - z, xx, c, h)
        share(1 - z, xx, h)
    relay_group(3)
    for h in range(2):
        wait_half(1 - z, far, c, h)
        share(1 - z, far, h)
    for xx in (x, left, right):
        for h in range(2):
            wait_half(1 - z, xx, 1 - c, h)

    def multiply_near(i, carry):
        multiply((1 - z) * 4 + (x + i + i // 2) % 4, 0, False)
        return carry

    lax.fori_loop(0, 3, multiply_near, 0)
    for h in range(2):
        wait_half(1 - z, far, 1 - c, h)
    multiply((1 - z) * 4 + far, 0, False)
    send_parts(0)
    wait_group(2)
    wait_group(3)
    multiply_all(z, 1, True)
    multiply_all(1 - z, 1, False)
    send_parts(1)
    fg_copy.wait_recv()
    for n in range(HALF // 2):
        kept = fg_all[pl.ds(pl.multiple_of(dp * 2048 + 64 * n, 64), 64), :]
        fg_ref[:, RADIX * n : RADIX * (n + 1)] = kept + fg_in[64 * n : 64 * (n + 1), :]

    for side in range(2):
        for d in range(2):
            wait_bytes(landed.at[d, :, pl.ds(32 * side, 32)], part_recv.at[d, side])
        columns = landed[0, :, pl.ds(32 * side, 32), :] + landed[1, :, pl.ds(32 * side, 32), :]
        columns = columns.reshape(256, 512)
        term = product(columns.T, columns)
        if side == 0:
            gram[...] = term
        else:
            gram[...] += term
    exchanges = []
    for i in range(4):
        view = (pl.ds(128 * i, 128), pl.ds(128 * i, 512 - 128 * i))
        copy = remote(gram.at[view], gram_in.at[view], gram_send.at[i], gram_recv.at[i], seq=sibling)
        launch(copy)
        exchanges.append(copy)
    current[...] = (landed[0] + landed[1]).reshape(512, 512).T
    for copy in exchanges:
        copy.wait_recv()
    diagonal = lax.broadcasted_iota(jnp.int32, (128, 128), 0) == lax.broadcasted_iota(jnp.int32, (128, 128), 1)
    trace = jnp.zeros((1, 1), F32)
    for i in range(4):
        block = gram[128 * i : 128 * (i + 1), 128 * i : 128 * (i + 1)]
        block = block + gram_in[128 * i : 128 * (i + 1), 128 * i : 128 * (i + 1)]
        trace = trace + jnp.sum(jnp.where(diagonal, block, 0.0), keepdims=True)
    scale = 1.0 / (jnp.sqrt(trace) + 1e-07)
    for i in range(4):
        for j in range(i, 4):
            at = (slice(128 * i, 128 * (i + 1)), slice(128 * j, 128 * (j + 1)))
            block = (gram[at] + gram_in[at]) * scale * scale
            gram_in[at] = block
            if j > i:
                gram_in[at[1], at[0]] = block.T
    current[...] = current[...] * scale

    def step(i, carry):
        gram_now = gram_in[...]
        mixer = COEF_B * gram_now + COEF_C * product(gram_now, gram_now)
        current[...] = COEF_A * current[...] + product(mixer, current[...])
        half_step = COEF_A * gram_now + product(mixer, gram_now)
        gram_in[...] = COEF_A * half_step + product(half_step, mixer)
        return carry

    lax.fori_loop(0, NS_STEPS - 1, step, 0)
    gram_now = gram_in[...]
    mixer = COEF_B * gram_now + COEF_C * product(gram_now, gram_now)
    current[...] = COEF_A * current[...] + product(mixer, current[...])
    is_owner = jnp.logical_and(owner == me, owner_dp == dp)
    away = remote(current, update_ref, final_sem.at[0], final_sem.at[1], seq=owner, dp=owner_dp)

    @pl.when(is_owner)
    def _():
        pltpu.make_async_copy(current, update_ref, final_sem.at[1]).start()

    @pl.when(jnp.logical_not(is_owner))
    def _():
        away.start()

    wait_bytes(update_ref, final_sem.at[1])

    @pl.when(jnp.logical_not(is_owner))
    def _():
        away.wait_send()

    for side in range(2):
        for j in range(2):
            away, _ = part_copy(j, side)

            @pl.when(jnp.logical_not(stays[j]))
            def _():
                away.wait_send()

    for i in range(GROUPS):
        wait_bytes(got.at[i, pl.ds(0, 63)], swap_send.at[i])
    for copy in pending:
        copy.wait_send()


def gradients(upstream, queries, keys, values, f, tokens):
    tabs = [jnp.asarray(t) for t in fourier_tables()]
    vm = pl.BlockSpec(memory_space=pltpu.VMEM)
    dma = pltpu.SemaphoreType.DMA
    square = pltpu.VMEM((512, 512), F32)
    return pl.pallas_call(
        gradient_kernel,
        out_shape=(
            jax.ShapeDtypeStruct((512, 512), F32),
            jax.ShapeDtypeStruct((64, HALF // 2 * RADIX), F32),
        ),
        in_specs=[vm] * 11,
        out_specs=[vm] * 2,
        scratch_shapes=[
            pltpu.VMEM((64, GROUPS, 3, GROUP, RADIX), BF16),
            pltpu.VMEM((GROUPS, 64, 3, GROUP, RADIX), BF16),
            pltpu.VMEM((8, 2, 4, RADIX, 1024), BF16),
            pltpu.VMEM((8, GROUPS, HALF, GROUP, RADIX), BF16),
            pltpu.VMEM((2, GROUPS, HALF, GROUP, RADIX), BF16),
            pltpu.VMEM((HALF * 64, RADIX), F32),
            pltpu.VMEM((HALF // 2 * 64, RADIX), F32),
            pltpu.VMEM((4, HALF * GROUP, RADIX), F32),
            pltpu.VMEM((2, HALF * GROUP, RADIX), F32),
            pltpu.VMEM((2, 8, 64, 512), F32),
            pltpu.VMEM((2, 8, 64, 512), F32),
            square, square, square,
            dma((GROUPS,)), dma((GROUPS,)), dma((GROUPS,)), dma((4, 2)), dma((6,)), dma((8, 2, 2)), dma((32,)), dma((8, GROUPS)), dma((28,)),
            dma((2,)), dma((2, 2)), dma((2, 2)), dma((4,)), dma((4,)), dma((2,)),
        ],
        compiler_params=pltpu.CompilerParams(
            collective_id=0, has_side_effects=True, vmem_limit_bytes=60 << 20
        ),
        name="gradients",
    )(upstream, queries, keys, values, f, tokens, *tabs)


def body(tokens, queries, keys, values, upstream, filters):
    update, filter_half = gradients(upstream[0], queries[0], keys[0], values[0], filters.T, tokens[0])
    filter_grad = filter_half.T
    return (update[None] * 32.0, filter_grad)


def solution(mesh):
    return jax.shard_map(
        body,
        mesh=mesh,
        in_specs=(
            P("dp", "seq", None),
            P("dp", "seq", None),
            P("dp", "seq", None),
            P("dp", "seq", None),
            P("dp", "seq", None),
            P(None, "seq"),
        ),
        out_specs=(P("seq", None, "dp"), P("dp", "seq")),
        check_vma=False,
    )
```
